256 devices in a mesh: tm: 8 (over x, core), rows: 32 (over y, z).
Axes of the slice: x: 4, y: 4, z: 8, core: 2. Of those that a mesh axis runs over, the one named last changes fastest.
Arguments:
- frames: bfloat16 [16, 32, 160, 384], P('tm', 'rows'), may hold values from -6 to 6
- first_cache: bfloat16 [2, 32, 160, 384], P(None, 'rows'), may hold values from -6 to 6
- second_cache: bfloat16 [2, 32, 160, 384], P(None, 'rows'), may hold values from -6 to 6
- first_gain: float32 [384], replicated, may hold values from 0.1 to 1.9
- second_gain: float32 [384], replicated, may hold values from 0.1 to 1.9
- first_weight: bfloat16 [3, 3, 3, 384, 384], P(None, None, None, None, 'rows'), may hold values from -0.0625 to 0.0625
- second_weight: bfloat16 [3, 3, 3, 384, 384], P(None, None, None, None, 'rows'), may hold values from -0.0625 to 0.0625
- upsample_weight: bfloat16 [3, 3, 384, 192], replicated, may hold values from -0.109375 to 0.109375
Outputs:
- upsampled: bfloat16 [16, 64, 320, 192], P('tm', 'rows')
The draws below stay inside these ranges and needn't reach their ends.
All inputs are finite; a program needn't handle non-finite values.
Results may differ from the reference program's by a relative error of at most 0.015.
Values may be sent and summed in bfloat16 or wider, within the bound.
A program may use at most 128 MiB of HBM per device.

```python
import jax
import jax.numpy as jnp
from jax import lax

C = 384
CO = 192
W = 160
TF = 16
H = 32


def steps_of(key, extent, cuts, low, largest):
    loudness, own = 1.0, jax.random.fold_in(key, 6)
    for position, shards_of in cuts:
        heights = jnp.exp(jax.random.uniform(jax.random.fold_in(own, position), (shards_of,), jnp.float32, low / len(cuts), largest / len(cuts)))
        loudness = loudness * jnp.repeat(heights, extent[position] // shards_of).reshape([-1 if axis == position else 1 for axis in range(len(extent))])
    return loudness


def bell_draw(own_key, extent, scale, reach, shards=(), kind=jnp.bfloat16):
    entries = jax.random.normal(own_key, extent, jnp.float32) * scale
    if len(shards) > 0:
        entries = steps_of(own_key, extent, shards, -0.22, 0.18) * entries
    return jnp.clip(entries, min=-reach, max=reach).astype(kind)


def setup_inputs(seed: int = 0) -> dict:
    key_list = jax.random.split(jax.random.key(seed), 9)
    return {
        "frames": bell_draw(key_list[0], (TF, H, W, C), 1.0, 6.0, ((0, 8), (1, 32))),
        "first_cache": bell_draw(key_list[1], (2, H, W, C), 1.0, 6.0, ((1, 32),)),
        "second_cache": bell_draw(key_list[2], (2, H, W, C), 1.0, 6.0, ((1, 32),)),
        "first_gain": jnp.clip(1.0 + 0.18 * jax.random.normal(key_list[3], (C,), jnp.float32), 0.1, 1.9),
        "second_gain": jnp.clip(1.0 + 0.18 * jax.random.normal(key_list[4], (C,), jnp.float32), 0.1, 1.9),
        "first_weight": bell_draw(key_list[5], (3, 3, 3, C, C), (27 * C) ** -0.5, 0.0625, ((4, 32),)),
        "second_weight": bell_draw(key_list[6], (3, 3, 3, C, C), (27 * C) ** -0.5, 0.0625, ((4, 32),)),
        "upsample_weight": bell_draw(key_list[7], (3, 3, C, CO), (9 * C) ** -0.5, 0.109375),
    }


def channel_norm(values, gain):
    values = values.astype(jnp.float32)
    scale = jax.lax.rsqrt(lax.optimization_barrier(jnp.mean(values * values, axis=-1, keepdims=True)) + 1e-06)
    return values * scale * gain

def causal_conv(cached, current, weight):
    joined = jnp.concatenate([cached, current], axis=0)
    padded = jnp.pad(joined, ((0, 0), (1, 1), (1, 1), (0, 0)))
    count = current.shape[0]
    height = current.shape[1]
    width = current.shape[2]
    total = jnp.zeros((count * height * width, weight.shape[-1]), jnp.float32)
    for time_tap in range(3):
        for row_tap in range(3):
            for col_tap in range(3):
                piece = padded[time_tap:time_tap + count, row_tap:row_tap + height, col_tap:col_tap + width]
                total = total + jnp.dot(piece.reshape(-1, piece.shape[-1]), weight[time_tap, row_tap, col_tap], preferred_element_type=jnp.float32)
    return total.reshape(count, height, width, weight.shape[-1])

def reference(frames, first_cache, second_cache, first_gain, second_gain, first_weight, second_weight, upsample_weight):
    first_input = jax.nn.silu(channel_norm(frames, first_gain)).astype(jnp.bfloat16)
    first_out = causal_conv(first_cache, first_input, first_weight).astype(jnp.bfloat16)
    second_input = jax.nn.silu(channel_norm(first_out, second_gain)).astype(jnp.bfloat16)
    block_out = (frames.astype(jnp.float32) + causal_conv(second_cache, second_input, second_weight)).astype(jnp.bfloat16)
    larger = jnp.repeat(jnp.repeat(block_out, 2, axis=1), 2, axis=2)
    padded = jnp.pad(larger, ((0, 0), (1, 1), (1, 1), (0, 0)))
    count = larger.shape[0]
    height = larger.shape[1]
    width = larger.shape[2]
    total = jnp.zeros((count * height * width, upsample_weight.shape[-1]), jnp.float32)
    for row_tap in range(3):
        for col_tap in range(3):
            piece = padded[:, row_tap:row_tap + height, col_tap:col_tap + width]
            total = total + jnp.dot(piece.reshape(-1, piece.shape[-1]), upsample_weight[row_tap, col_tap], preferred_element_type=jnp.float32)
    return total.reshape(count, height, width, upsample_weight.shape[-1]).astype(jnp.bfloat16)
```

```python
import jax
import jax.numpy as jnp
from jax import lax
from jax.experimental import pallas as pl
from jax.experimental.pallas import tpu as pltpu
from jax.sharding import PartitionSpec as P

BF = jnp.bfloat16
F32 = jnp.float32
NT = (((1,), (1,)), ((), ()))
W = 160
C = 384
CO = 192
ND = 21
NQ = 5
NU = ND + NQ
NC = 41
TAPS = (((0,), (1, 2)), ((0, 1), (2,)))


def mod(a, n):
    return lax.rem(a + n, n)


def kernel(
    frames,
    cache0,
    cache1,
    gain0,
    gain1,
    win0,
    win1,
    up,
    out,
    zb0,
    zb1,
    w0,
    w1,
    xs0,
    xs1,
    bs,
    acc,
    cw,
    ph,
    il,
    ssem,
    rsem,
):
    tm = lax.axis_index("tm")
    r = lax.axis_index("rows")
    x, c = tm // 2, tm % 2
    y, z = r // 8, r % 8
    zdev = lambda d: (tm, y * 8 + mod(z + d, 8))
    ydev = lambda d: (tm, mod(y + d, 4) * 8 + z)
    xdev = lambda d: (mod(x + d, 4) * 2 + c, r)
    tdev = lambda d: (mod(tm + d, 8), r)
    rdev = lambda d: (tm, mod(r + d, 32))
    pair = (x * 2 + 1 - c, r)

    index = {}
    sends = []

    def copy(key, src, dst, dev):
        n = index.setdefault(key, len(index))
        return pltpu.make_async_remote_copy(
            src_ref=src,
            dst_ref=dst,
            send_sem=ssem.at[n],
            recv_sem=rsem.at[n],
            device_id=dev,
            device_id_type=pl.DeviceIdType.MESH,
        )

    def send(key, src, dev, dst=None, when=None):
        dst = src if dst is None else dst

        def go():
            copy(key, src, dst, dev).start()

        if when is None:
            go()
        else:
            pl.when(when)(go)
        sends.append((key, src, dst, dev, when))

    def recv(key, dst, when=None):
        def go():
            copy(key, dst, dst, pair).wait_recv()

        if when is None:
            go()
        else:
            pl.when(when)(go)

    zbs, ws, wins, xss = (zb0, zb1), (w0, w1), (win0, win1), (xs0, xs1)
    caches, gains = (cache0, cache1), (gain0, gain1)

    def prepare(v):
        zb, win = zbs[v], wins[v]
        zb[z] = jnp.zeros((NU, 16, 128), BF)

        def body(n, _):
            local = jnp.where(n < ND, n, n + NQ * x)
            u = jnp.where(c == 0, local, jnp.where(local == 40, 40, 41 + local))
            lane = pl.multiple_of((u % 3) * 128, 128)
            zb[z, n, 0:12, :] = win[u // 3, :, pl.ds(lane, 128)]
            return 0

        lax.fori_loop(0, NU, body, 0)

    def zblock(v, d):
        return zbs[v].at[mod(z + d, 8)]

    def zstart(v, s):
        send(("zf", v, s), zblock(v, 1 - s), zdev(1))
        if s < 4:
            send(("zb", v, s), zblock(v, s - 1), zdev(-1))

    def zwait(v, s):
        recv(("zf", v, s), zblock(v, -s))
        if s < 4:
            recv(("zb", v, s), zblock(v, s))

    row = lax.broadcasted_iota(jnp.int32, (96, 128), 0)
    col = lax.broadcasted_iota(jnp.int32, (96, 128), 1)
    squeeze = jnp.where(row + 4 * (row // 12) == col, 1.0, 0.0).astype(BF)
    ybase = lambda d: pl.multiple_of(mod(y + d, 4) * 96, 96)
    slot = lambda n: 41 * c + jnp.where(n < ND, n, n + NQ * x)

    def assemble(v, lo, hi):
        zb, w = zbs[v], ws[v]

        def one(n):
            w[slot(n), pl.ds(ybase(0), 96), :] = jnp.dot(
                squeeze, zb[:, n].reshape(128, 128), preferred_element_type=F32
            ).astype(BF)

        def body(n, _):
            one(lo + 2 * n)
            one(lo + 2 * n + 1)
            return 0

        lax.fori_loop(0, (hi - lo) // 2, body, 0)
        if (hi - lo) % 2:
            one(jnp.int32(hi - 1))

    dbase = 41 * c
    qbase = lambda d: 41 * c + ND + NQ * mod(x + d, 4)
    segment = {"q": (qbase(0), NQ, 3), "d": (dbase, ND, 11)}

    def yview(v, g, d, part):
        base, count, cut = segment[g]
        lo, n = ((0, count), (0, cut), (cut, count - cut))[part]
        return ws[v].at[pl.ds(base + lo, n), pl.ds(ybase(d), 96), :]

    def ystart1(v, g):
        send(("yf1", v, g), yview(v, g, 0, 0), ydev(1))
        send(("yb1", v, g), yview(v, g, 0, 0), ydev(-1))

    def ystart2(v, g):
        recv(("yf1", v, g), yview(v, g, -1, 0))
        send(("yf2", v, g), yview(v, g, -1, 1), ydev(1))
        recv(("yb1", v, g), yview(v, g, 1, 0))
        send(("yb2", v, g), yview(v, g, 1, 2), ydev(-1))

    def ywait2(v, g):
        recv(("yf2", v, g), yview(v, g, -2, 1))
        recv(("yb2", v, g), yview(v, g, 2, 2))

    def xview(v, d, part):
        lo, n = ((0, NQ), (0, 3), (3, 2))[part]
        return ws[v].at[pl.ds(qbase(d) + lo, n)]

    def cview(v, core, lo, n):
        return ws[v].at[pl.ds(41 * core + lo, n)]

    def xstart1(v):
        send(("xf1", v), xview(v, 0, 0), xdev(1))
        send(("xb1", v), xview(v, 0, 0), xdev(-1))

    def xstart2(v):
        recv(("xf1", v), xview(v, -1, 0))
        send(("xf2", v), xview(v, -1, 1), xdev(1))
        recv(("xb1", v), xview(v, 1, 0))
        send(("xb2", v), xview(v, 1, 2), xdev(-1))

    def xwait2(v):
        recv(("xf2", v), xview(v, -2, 1))
        recv(("xb2", v), xview(v, 2, 2))

    def handd(v):
        send(("cd", v), cview(v, c, 0, ND), pair)

    def handq(v):
        send(("cq", v), cview(v, c, ND, NC - ND), pair)

    def handwait(v):
        recv(("cd", v), cview(v, 1 - c, 0, ND))
        recv(("cq", v), cview(v, 1 - c, ND, NC - ND))

    def normed(v, values):
        scale = lax.rsqrt(jnp.mean(values * values, axis=-1, keepdims=True) + 1e-06)
        return jax.nn.silu(values * scale * gains[v][...]).astype(BF)

    inner_lo, inner_hi, later, first = r > 0, r < 31, tm < 7, tm == 0

    def halo_start(v):
        xs = xss[v]
        own = xs.at[1, 1, pl.ds(2, 2)]
        send(("up", v), own, rdev(1), xs.at[1, 0, pl.ds(2, 2)], inner_hi)
        send(("dn", v), own, rdev(-1), xs.at[1, 2, pl.ds(2, 2)], inner_lo)
        send(("t1", v), own, tdev(1), xs.at[1, 1, pl.ds(0, 2)], later)

    def cache_start(v):
        xs = xss[v]

        @pl.when(first)
        def _():
            xs[1, 1, 0:2] = caches[v][...]

        old = xs.at[1, 1, pl.ds(0, 2)]
        send(("cu", v), old, rdev(1), xs.at[1, 0, pl.ds(0, 2)], first & inner_hi)
        send(("cn", v), old, rdev(-1), xs.at[1, 2, pl.ds(0, 2)], first & inner_lo)

        @pl.when(r == 0)
        def _():
            xs[1, 0] = jnp.zeros((4, W, C), BF)

        @pl.when(r == 31)
        def _():
            xs[1, 2] = jnp.zeros((4, W, C), BF)

    def halo_pass(v):
        xs = xss[v]
        low, high = xs.at[1, 0, pl.ds(2, 2)], xs.at[1, 2, pl.ds(2, 2)]
        recv(("up", v), low, inner_lo)
        send(("t0", v), low, tdev(1), xs.at[1, 0, pl.ds(0, 2)], later & inner_lo)
        recv(("dn", v), high, inner_hi)
        send(("t2", v), high, tdev(1), xs.at[1, 2, pl.ds(0, 2)], later & inner_hi)

    def halo_wait(v):
        xs = xss[v]
        old = [xs.at[1, j, pl.ds(0, 2)] for j in range(3)]
        recv(("t1", v), old[1], tm > 0)
        recv(("t0", v), old[0], (tm > 0) & inner_lo)
        recv(("t2", v), old[2], (tm > 0) & inner_hi)
        recv(("cu", v), old[0], first & inner_lo)
        recv(("cn", v), old[2], first & inner_hi)

    def shift(buf, j, f):
        v = buf[1, j, f].astype(F32)
        at = lax.broadcasted_iota(jnp.int32, v.shape, 0)
        buf[0, j, f] = jnp.where(at == 0, 0.0, pltpu.roll(v, 1, 0)).astype(BF)
        buf[2, j, f] = jnp.where(at == W - 1, 0.0, pltpu.roll(v, W - 1, 0)).astype(BF)

    def shifts(buf, js, f0, n):
        for j in js:

            def body(f, _):
                shift(buf, j, f0 + f)
                return 0

            lax.fori_loop(0, n, body, 0)

    def conv(v, lo, hi):
        xs, w = xss[v], ws[v]

        def body(ij, _):
            i, j = ij // 3, ij % 3
            lhs = jnp.concatenate(
                [xs[k, j, pl.ds(i, 2)].reshape(2 * W, C) for k in range(3)], axis=1
            )
            rhs = jnp.concatenate([w[9 * ij + u] for u in range(9)], axis=1)
            acc[...] += lax.dot_general(lhs, rhs, NT, preferred_element_type=F32)
            return 0

        lax.fori_loop(lo, hi, body, 0)

    def combine():
        for a in range(2):
            for p in range(2):
                for b in range(2):
                    for q in range(2):
                        total = sum(
                            up[j, k].astype(F32) for j in TAPS[a][p] for k in TAPS[b][q]
                        )
                        cw[a, p, b, q] = total.astype(BF)

    def phase(a, b, p):
        lhs = jnp.concatenate(
            [bs[b + q, a + p].reshape(2 * W, C) for q in range(2)], axis=1
        )
        rhs = jnp.concatenate([cw[a, p, b, q] for q in range(2)], axis=1)
        return lax.dot_general(lhs, rhs, NT, preferred_element_type=F32)

    prepare(0)
    barrier = pltpu.get_barrier_semaphore()
    for near in (zdev, ydev, xdev, tdev, rdev):
        for d in (1, -1):
            pl.semaphore_signal(
                barrier, inc=1, device_id=near(d), device_id_type=pl.DeviceIdType.MESH
            )
    pl.semaphore_wait(barrier, 10)

    zstart(0, 1)
    xs0[1, 1, 2:4] = normed(0, frames[...].astype(F32).reshape(2 * W, C)).reshape(2, W, C)
    halo_start(0)
    cache_start(0)
    zwait(0, 1)
    zstart(0, 2)
    cache_start(1)
    prepare(1)
    zwait(0, 2)
    zstart(0, 3)
    shifts(xs0, (1,), 2, 2)
    halo_pass(0)
    zwait(0, 3)
    zstart(0, 4)
    combine()
    zwait(0, 4)
    zstart(1, 1)
    assemble(0, ND, NU)
    ystart1(0, "q")
    assemble(0, 0, ND)
    ystart1(0, "d")
    zwait(1, 1)
    zstart(1, 2)
    ystart2(0, "q")
    zwait(1, 2)
    zstart(1, 3)
    ywait2(0, "q")
    xstart1(0)
    zwait(1, 3)
    zstart(1, 4)
    halo_wait(0)
    shifts(xs0, (0, 2), 2, 2)
    shifts(xs0, (0, 1, 2), 0, 2)
    zwait(1, 4)
    ystart2(0, "d")
    assemble(1, ND, NU)
    ystart1(1, "q")
    assemble(1, 0, ND)
    ystart1(1, "d")
    xstart2(0)
    ywait2(0, "d")
    handd(0)
    ystart2(1, "q")
    ywait2(1, "q")
    xwait2(0)
    handq(0)
    xstart1(1)
    acc[...] = jnp.zeros_like(acc)
    handwait(0)
    conv(0, 0, 9)
    xs1[1, 1, 2:4] = normed(1, acc[...].astype(BF).astype(F32)).reshape(2, W, C)
    halo_start(1)
    ystart2(1, "d")
    xstart2(1)
    shifts(xs1, (1,), 2, 2)
    halo_pass(1)
    ywait2(1, "d")
    handd(1)
    xwait2(1)
    handq(1)
    halo_wait(1)
    shifts(xs1, (0, 2), 2, 2)
    shifts(xs1, (0, 1, 2), 0, 2)
    acc[...] = frames[...].astype(F32).reshape(2 * W, C)
    handwait(1)
    conv(1, 0, 9)

    bs[1, 1] = acc[...].astype(BF).reshape(2, W, C)
    send("bu", bs.at[1, 1], rdev(1), bs.at[1, 0], inner_hi)
    send("bd", bs.at[1, 1], rdev(-1), bs.at[1, 2], inner_lo)

    @pl.when(r == 0)
    def _():
        bs[1, 0] = jnp.zeros((2, W, C), BF)

    @pl.when(r == 31)
    def _():
        bs[1, 2] = jnp.zeros((2, W, C), BF)

    shifts(bs, (1,), 0, 2)
    for a in range(2):
        for b in range(2):
            ph[a, b] = phase(a, b, 1 - a)
    recv("bu", bs.at[1, 0], inner_lo)
    recv("bd", bs.at[1, 2], inner_hi)
    shifts(bs, (0, 2), 0, 2)
    for a in range(2):
        for b in range(2):
            total = ph[a, b] + phase(a, b, a)
            for f in range(2):
                part = total[f * W : (f + 1) * W]
                il[f, pl.ds(b, W, stride=2), :] = part[:, :128]
                il[2 + f, pl.ds(b, W, stride=2), 0:64] = part[:, 128:]
        for f in range(2):
            out[f, a, :, 0:128] = il[f].astype(BF)
            out[f, a, :, 128:192] = il[2 + f, :, 0:64].astype(BF)

    for key, src, dst, dev, when in sends:
        done = lambda k=key, s=src, d=dst, e=dev: copy(k, s, d, e).wait_send()
        if when is None:
            done()
        else:
            pl.when(when)(done)


def shards(frames, cache0, cache1, gain0, gain1, first, second, upsample):
    vmem = pl.BlockSpec(memory_space=pltpu.VMEM)
    block = lambda v: v.reshape(2, W, C)
    flip = lambda v: jnp.swapaxes(v, 3, 4).reshape(27, 12, C)
    return pl.pallas_call(
        kernel,
        out_shape=jax.ShapeDtypeStruct((2, 2, 2 * W, CO), BF),
        in_specs=[vmem] * 8,
        out_specs=vmem,
        scratch_shapes=[
            pltpu.VMEM((8, NU, 16, 128), BF),
            pltpu.VMEM((8, NU, 16, 128), BF),
            pltpu.VMEM((2 * NC, C, 128), BF),
            pltpu.VMEM((2 * NC, C, 128), BF),
            pltpu.VMEM((3, 3, 4, W, C), BF),
            pltpu.VMEM((3, 3, 4, W, C), BF),
            pltpu.VMEM((3, 3, 2, W, C), BF),
            pltpu.VMEM((2 * W, C), F32),
            pltpu.VMEM((2, 2, 2, 2, CO, C), BF),
            pltpu.VMEM((2, 2, 2 * W, CO), F32),
            pltpu.VMEM((4, 2 * W, 128), F32),
            pltpu.SemaphoreType.DMA((64,)),
            pltpu.SemaphoreType.DMA((64,)),
        ],
        compiler_params=pltpu.CompilerParams(
            collective_id=0, has_side_effects=True, vmem_limit_bytes=60 << 20
        ),
    )(
        block(frames),
        block(cache0),
        block(cache1),
        gain0.reshape(1, C),
        gain1.reshape(1, C),
        flip(first),
        flip(second),
        jnp.swapaxes(upsample, 2, 3),
    )


def solution(mesh):
    in_specs = (
        P("tm", "rows", None, None),
        P(None, "rows", None, None),
        P(None, "rows", None, None),
        P(),
        P(),
        P(None, None, None, None, "rows"),
        P(None, None, None, None, "rows"),
        P(),
    )
    out_specs = P("tm", "rows", None, None)
    return jax.shard_map(shards, mesh=mesh, in_specs=in_specs, out_specs=out_specs, check_vma=False)
```

```python
import jax
import jax.numpy as jnp
from jax import lax
from jax.experimental import pallas as pl
from jax.experimental.pallas import tpu as pltpu
from jax.sharding import PartitionSpec as P

BF = jnp.bfloat16
F32 = jnp.float32
NT = (((1,), (1,)), ((), ()))
W = 160
C = 384
CO = 192
ND = (21, 25)
NQ = (5, 4)
NC = 41
NB = 9
CUTS = ((12, 0), (9, 7))
TAPS = (((0,), (1, 2)), ((0, 1), (2,)))


def mod(a, n):
    return lax.rem(a + n, n)


def kernel(
    frames,
    cache0,
    cache1,
    gain0,
    gain1,
    win0,
    win1,
    up,
    out,
    zb0,
    zb1,
    w0,
    w1,
    xs0,
    xs1,
    bs,
    acc,
    cw,
    ph,
    il,
    ssem,
    rsem,
):
    tm = lax.axis_index("tm")
    r = lax.axis_index("rows")
    x, c = tm // 2, tm % 2
    y, z = r // 8, r % 8
    zdev = lambda d: (tm, y * 8 + mod(z + d, 8))
    ydev = lambda d: (tm, mod(y + d, 4) * 8 + z)
    xdev = lambda d: (mod(x + d, 4) * 2 + c, r)
    tdev = lambda d: (mod(tm + d, 8), r)
    rdev = lambda d: (tm, mod(r + d, 32))
    pair = (x * 2 + 1 - c, r)

    index = {}
    sends = []

    def copy(key, src, dst, dev):
        n = index.setdefault(key, len(index))
        return pltpu.make_async_remote_copy(
            src_ref=src,
            dst_ref=dst,
            send_sem=ssem.at[n],
            recv_sem=rsem.at[n],
            device_id=dev,
            device_id_type=pl.DeviceIdType.MESH,
        )

    def send(key, src, dev, dst=None, when=None):
        dst = src if dst is None else dst

        def go():
            copy(key, src, dst, dev).start()

        if when is None:
            go()
        else:
            pl.when(when)(go)
        sends.append((key, src, dst, dev, when))

    def recv(key, dst, when=None):
        def go():
            copy(key, dst, dst, pair).wait_recv()

        if when is None:
            go()
        else:
            pl.when(when)(go)

    zbs, ws, wins, xss = (zb0, zb1), (w0, w1), (win0, win1), (xs0, xs1)
    caches, gains = (cache0, cache1), (gain0, gain1)

    chunks = []
    for d, q, (nc, ne) in zip(ND, NQ, CUTS):
        chunks.append(
            {
                "b": (0, NB),
                "c": (NB, nc),
                "e": (NB + nc, ne),
                "r": (NB, nc + ne),
                "q": (d, q),
            }
        )

    def unit(v, n):
        local = jnp.where(n < ND[v], n, n + NQ[v] * x)
        second = jnp.where(
            local < 18,
            45 + local,
            jnp.where(
                local < 21,
                23 + local,
                jnp.where(local == 21, 44, jnp.where(local == 40, 40, 41 + local)),
            ),
        )
        return jnp.where(c == 0, local, second)

    def prepare(v):
        zb, win = zbs[v], wins[v]
        zb[z] = jnp.zeros((ND[v] + NQ[v], 16, 128), BF)

        def body(n, _):
            u = unit(v, n)
            lane = pl.multiple_of((u % 3) * 128, 128)
            zb[z, n, 0:12, :] = win[u // 3, :, pl.ds(lane, 128)]
            return 0

        lax.fori_loop(0, ND[v] + NQ[v], body, 0)

    def split(v, g, part):
        lo, n = chunks[v][g]
        cut = (n + 1) // 2
        return ((lo, n), (lo, cut), (lo + cut, n - cut))[part]

    def zview(v, g, d, part=0):
        return zbs[v].at[mod(z + d, 8), pl.ds(*split(v, g, part))]

    def zstart(v, g):
        for d in (2, -2, 1, -1):
            send(("z", v, g, d), zview(v, g, 0), zdev(d))

    def zpass(v, g):
        for d in (2, -2):
            part = 1 if d > 0 else 2
            recv(("z", v, g, d), zview(v, g, -d))
            send(("z", v, g, 2 * d), zview(v, g, -d, part), zdev(d))
            send(("z", v, g, 3 * d // 2), zview(v, g, -d), zdev(d // 2))

    def zwait(v, g):
        for d in (1, -1, 3, -3):
            recv(("z", v, g, d), zview(v, g, -d))
        for d in (4, -4):
            recv(("z", v, g, d), zview(v, g, -d, 1 if d > 0 else 2))

    row = lax.broadcasted_iota(jnp.int32, (96, 128), 0)
    col = lax.broadcasted_iota(jnp.int32, (96, 128), 1)
    squeeze = jnp.where(row + 4 * (row // 12) == col, 1.0, 0.0).astype(BF)
    ybase = lambda d: pl.multiple_of(mod(y + d, 4) * 96, 96)
    qbase = lambda v, core, d: 41 * core + ND[v] + NQ[v] * mod(x + d, 4)

    def base(v, g, core, d=0):
        return qbase(v, core, d) if g == "q" else 41 * core + chunks[v][g][0]

    def assemble(v, g):
        lo, count = chunks[v][g]
        blocks = [zbs[v][:, lo + n].reshape(128, 128) for n in range(count)]
        rows = jnp.dot(
            squeeze, jnp.concatenate(blocks, axis=1), preferred_element_type=F32
        ).astype(BF)
        first = base(v, g, c)
        for n in range(count):
            ws[v][first + n, pl.ds(ybase(0), 96), :] = rows[:, 128 * n : 128 * n + 128]

    def yview(v, g, d, part):
        lo, n = split(v, g, part)
        lo = lo - chunks[v][g][0]
        return ws[v].at[pl.ds(base(v, g, c) + lo, n), pl.ds(ybase(d), 96), :]

    def ystart(v, g):
        send(("yf1", v, g), yview(v, g, 0, 0), ydev(1))
        send(("yb1", v, g), yview(v, g, 0, 0), ydev(-1))

    def ypass(v, g):
        recv(("yf1", v, g), yview(v, g, -1, 0))
        send(("yf2", v, g), yview(v, g, -1, 1), ydev(1))
        recv(("yb1", v, g), yview(v, g, 1, 0))
        send(("yb2", v, g), yview(v, g, 1, 2), ydev(-1))

    def ywait(v, g):
        recv(("yf2", v, g), yview(v, g, -2, 1))
        recv(("yb2", v, g), yview(v, g, 2, 2))

    def xview(v, d, part):
        lo, n = ((0, 1), (1, NQ[v] - 1))[part - 1]
        return ws[v].at[pl.ds(qbase(v, c, d) + lo, n)]

    def xstart(v):
        for first in (1, 2):
            send(("xf", v, first), xview(v, 0, first), xdev(1))
            send(("xb", v, 3 - first), xview(v, 0, 3 - first), xdev(-1))

    def xpass(v, d):
        key, part = ("xf", 1) if d > 0 else ("xb", 2)
        recv((key, v, part), xview(v, -d, part))
        send((key, v, 3), xview(v, -d, part), xdev(d))

    def xsides(v):
        recv(("xf", v, 2), xview(v, -1, 2))
        recv(("xb", v, 1), xview(v, 1, 1))

    def xwait(v):
        recv(("xf", v, 3), xview(v, -2, 1))
        recv(("xb", v, 3), xview(v, 2, 2))

    def cview(v, g, core, d=0):
        return ws[v].at[pl.ds(base(v, g, core, d), chunks[v][g][1])]

    def hand(v, g, d=0):
        send(("c", v, g, d), cview(v, g, c, d), pair)

    def taken(v, g, d=0):
        recv(("c", v, g, d), cview(v, g, 1 - c, d))

    def alltaken(v):
        for d in (0, 1, -1, 2):
            taken(v, "q", d)

    def normed(v, values):
        scale = lax.rsqrt(jnp.mean(values * values, axis=-1, keepdims=True) + 1e-06)
        return jax.nn.silu(values * scale * gains[v][...]).astype(BF)

    inner_lo, inner_hi, later, first = r > 0, r < 31, tm < 7, tm == 0

    def halo_row(v):
        xs = xss[v]
        own = xs.at[1, 1, pl.ds(2, 2)]
        send(("t1", v), own, tdev(1), xs.at[1, 1, pl.ds(0, 2)], later)

    def halo_start(v):
        xs = xss[v]
        own = xs.at[1, 1, pl.ds(2, 2)]
        send(("up", v), own, rdev(1), xs.at[1, 0, pl.ds(2, 2)], inner_hi)
        send(("dn", v), own, rdev(-1), xs.at[1, 2, pl.ds(2, 2)], inner_lo)
        away = later & (c == 1)
        below, above = (mod(tm + 1, 8), mod(r + 1, 32)), (mod(tm + 1, 8), mod(r - 1, 32))
        send(("t0", v), own, below, xs.at[1, 0, pl.ds(0, 2)], away & inner_hi)
        send(("t2", v), own, above, xs.at[1, 2, pl.ds(0, 2)], away & inner_lo)

    def cache_start(v):
        xs = xss[v]

        @pl.when(first)
        def _():
            xs[1, 1, 0:2] = caches[v][...]

        old = xs.at[1, 1, pl.ds(0, 2)]
        send(("cu", v), old, rdev(1), xs.at[1, 0, pl.ds(0, 2)], first & inner_hi)
        send(("cn", v), old, rdev(-1), xs.at[1, 2, pl.ds(0, 2)], first & inner_lo)

        @pl.when(r == 0)
        def _():
            xs[1, 0] = jnp.zeros((4, W, C), BF)

        @pl.when(r == 31)
        def _():
            xs[1, 2] = jnp.zeros((4, W, C), BF)

    def halo_pass(v):
        xs = xss[v]
        low, high = xs.at[1, 0, pl.ds(2, 2)], xs.at[1, 2, pl.ds(2, 2)]
        recv(("up", v), low, inner_lo)
        send(("t0", v), low, tdev(1), xs.at[1, 0, pl.ds(0, 2)], (c == 0) & inner_lo)
        recv(("dn", v), high, inner_hi)
        send(("t2", v), high, tdev(1), xs.at[1, 2, pl.ds(0, 2)], (c == 0) & inner_hi)

    def halo_wait(v):
        xs = xss[v]
        old = [xs.at[1, j, pl.ds(0, 2)] for j in range(3)]
        recv(("t1", v), old[1], tm > 0)
        recv(("t0", v), old[0], (tm > 0) & inner_lo)
        recv(("t2", v), old[2], (tm > 0) & inner_hi)
        recv(("cu", v), old[0], first & inner_lo)
        recv(("cn", v), old[2], first & inner_hi)

    def shift(buf, j, f):
        v = buf[1, j, f].astype(F32)
        at = lax.broadcasted_iota(jnp.int32, v.shape, 0)
        buf[0, j, f] = jnp.where(at == 0, 0.0, pltpu.roll(v, 1, 0)).astype(BF)
        buf[2, j, f] = jnp.where(at == W - 1, 0.0, pltpu.roll(v, W - 1, 0)).astype(BF)

    def shifts(buf, js, f0, n):
        for j in js:

            def body(f, _):
                shift(buf, j, f0 + f)
                return 0

            lax.fori_loop(0, n, body, 0)

    def conv(v, *pieces):
        xs, w = xss[v], ws[v]

        def body(n, _):
            ij = jnp.int32(pieces[0])
            for m in range(1, len(pieces)):
                ij = jnp.where(n == m, pieces[m], ij)
            i, j = ij // 3, ij % 3
            low = 9 * ij - jnp.where((ij == 5) | (ij == 6), 4, 0)
            high = low + jnp.where(ij == 4, 18, 0)
            lhs = jnp.concatenate(
                [xs[k, j, pl.ds(i, 2)].reshape(2 * W, C) for k in range(3)], axis=1
            )
            rhs = jnp.concatenate([w[(low if u < 5 else high) + u] for u in range(9)], axis=1)
            acc[...] += lax.dot_general(lhs, rhs, NT, preferred_element_type=F32)
            return 0

        lax.fori_loop(0, len(pieces), body, 0)

    def combine():
        for a in range(2):
            for p in range(2):
                for b in range(2):
                    for q in range(2):
                        total = sum(
                            up[j, k].astype(F32) for j in TAPS[a][p] for k in TAPS[b][q]
                        )
                        cw[a, p, b, q] = total.astype(BF)

    def phase(a, b, p):
        lhs = jnp.concatenate(
            [bs[b + q, a + p].reshape(2 * W, C) for q in range(2)], axis=1
        )
        rhs = jnp.concatenate([cw[a, p, b, q] for q in range(2)], axis=1)
        return lax.dot_general(lhs, rhs, NT, preferred_element_type=F32)

    barrier = pltpu.get_barrier_semaphore()
    near = [f(d) for f in (zdev, ydev, xdev, tdev, rdev) for d in (1, -1)]
    near += [zdev(2), zdev(-2)]
    near += [(mod(tm + d, 8), mod(r + e, 32)) for d in (1, -1) for e in (1, -1)]
    for dev in near:
        pl.semaphore_signal(barrier, inc=1, device_id=dev, device_id_type=pl.DeviceIdType.MESH)
    prepare(0)
    pl.semaphore_wait(barrier, len(near))

    zstart(0, "q")
    xs0[1, 1, 2:4] = normed(0, frames[...].astype(F32).reshape(2 * W, C)).reshape(2, W, C)
    halo_row(0)
    zpass(0, "q")
    zstart(0, "b")
    zstart(0, "c")
    zwait(0, "q")
    assemble(0, "q")
    ystart(0, "q")
    zpass(0, "b")
    prepare(1)
    zpass(0, "c")
    zwait(0, "b")
    assemble(0, "b")
    ypass(0, "q")
    ystart(0, "b")
    zwait(0, "c")
    assemble(0, "c")
    ystart(0, "c")
    ywait(0, "q")
    xstart(0)
    hand(0, "q", 0)
    zstart(1, "q")
    zstart(1, "b")
    halo_start(0)
    cache_start(0)
    zstart(1, "r")
    ypass(0, "b")
    xpass(0, 1)
    zpass(1, "q")
    zpass(1, "b")
    shifts(xs0, (1,), 2, 2)
    ypass(0, "c")
    zwait(1, "q")
    assemble(1, "q")
    ystart(1, "q")
    xpass(0, -1)
    ywait(0, "b")
    hand(0, "b")
    halo_pass(0)
    zwait(1, "b")
    assemble(1, "b")
    ystart(1, "b")
    ywait(0, "c")
    hand(0, "c")
    xsides(0)
    hand(0, "q", 1)
    hand(0, "q", -1)
    zpass(1, "r")
    ypass(1, "q")
    acc[...] = jnp.zeros_like(acc)
    halo_wait(0)
    shifts(xs0, (0, 2), 2, 2)
    shifts(xs0, (0, 1, 2), 0, 2)
    taken(0, "b")
    conv(0, 0, 5)
    xwait(0)
    hand(0, "q", 2)
    ywait(1, "q")
    xstart(1)
    hand(1, "q", 0)
    taken(0, "c")
    conv(0, 1, 6)
    zwait(1, "r")
    assemble(1, "c")
    ystart(1, "c")
    assemble(1, "e")
    ystart(1, "e")
    ypass(1, "b")
    alltaken(0)
    conv(0, 2, 3, 4, 7, 8)
    xs1[1, 1, 2:4] = normed(1, acc[...].astype(BF).astype(F32)).reshape(2, W, C)
    halo_row(1)
    halo_start(1)
    cache_start(1)
    xpass(1, 1)
    acc[...] = frames[...].astype(F32).reshape(2 * W, C)
    shifts(xs1, (1,), 2, 2)
    xpass(1, -1)
    ypass(1, "c")
    combine()
    ywait(1, "b")
    hand(1, "b")
    xsides(1)
    hand(1, "q", 1)
    hand(1, "q", -1)
    halo_pass(1)
    ypass(1, "e")
    xwait(1)
    hand(1, "q", 2)
    ywait(1, "c")
    hand(1, "c")
    halo_wait(1)
    shifts(xs1, (0, 2), 2, 2)
    shifts(xs1, (0, 1, 2), 0, 2)
    taken(1, "b")
    conv(1, 0, 5)
    ywait(1, "e")
    hand(1, "e")
    taken(1, "c")
    conv(1, 1, 6)
    alltaken(1)
    conv(1, 3, 8)
    taken(1, "e")
    conv(1, 2, 4, 7)

    bs[1, 1] = acc[...].astype(BF).reshape(2, W, C)
    send("bu", bs.at[1, 1], rdev(1), bs.at[1, 0], inner_hi)
    send("bd", bs.at[1, 1], rdev(-1), bs.at[1, 2], inner_lo)

    @pl.when(r == 0)
    def _():
        bs[1, 0] = jnp.zeros((2, W, C), BF)

    @pl.when(r == 31)
    def _():
        bs[1, 2] = jnp.zeros((2, W, C), BF)

    shifts(bs, (1,), 0, 2)
    for a in range(2):
        for b in range(2):
            ph[a, b] = phase(a, b, 1 - a)
    recv("bu", bs.at[1, 0], inner_lo)
    recv("bd", bs.at[1, 2], inner_hi)
    shifts(bs, (0, 2), 0, 2)
    for a in range(2):
        for b in range(2):
            total = ph[a, b] + phase(a, b, a)
            for f in range(2):
                part = total[f * W : (f + 1) * W]
                il[f, pl.ds(b, W, stride=2), :] = part[:, :128]
                il[2 + f, pl.ds(b, W, stride=2), 0:64] = part[:, 128:]
        for f in range(2):
            out[f, a, :, 0:128] = il[f].astype(BF)
            out[f, a, :, 128:192] = il[2 + f, :, 0:64].astype(BF)

    for key, src, dst, dev, when in sends:
        done = lambda k=key, s=src, d=dst, e=dev: copy(k, s, d, e).wait_send()
        if when is None:
            done()
        else:
            pl.when(when)(done)


def shards(frames, cache0, cache1, gain0, gain1, first, second, upsample):
    vmem = pl.BlockSpec(memory_space=pltpu.VMEM)
    block = lambda v: v.reshape(2, W, C)
    flip = lambda v: jnp.swapaxes(v, 3, 4).reshape(27, 12, C)
    return pl.pallas_call(
        kernel,
        out_shape=jax.ShapeDtypeStruct((2, 2, 2 * W, CO), BF),
        in_specs=[vmem] * 8,
        out_specs=vmem,
        scratch_shapes=[
            pltpu.VMEM((8, ND[0] + NQ[0], 16, 128), BF),
            pltpu.VMEM((8, ND[1] + NQ[1], 16, 128), BF),
            pltpu.VMEM((2 * NC, C, 128), BF),
            pltpu.VMEM((2 * NC, C, 128), BF),
            pltpu.VMEM((3, 3, 4, W, C), BF),
            pltpu.VMEM((3, 3, 4, W, C), BF),
            pltpu.VMEM((3, 3, 2, W, C), BF),
            pltpu.VMEM((2 * W, C), F32),
            pltpu.VMEM((2, 2, 2, 2, CO, C), BF),
            pltpu.VMEM((2, 2, 2 * W, CO), F32),
            pltpu.VMEM((4, 2 * W, 128), F32),
            pltpu.SemaphoreType.DMA((136,)),
            pltpu.SemaphoreType.DMA((136,)),
        ],
        compiler_params=pltpu.CompilerParams(
            collective_id=0, has_side_effects=True, vmem_limit_bytes=60 << 20
        ),
    )(
        block(frames),
        block(cache0),
        block(cache1),
        gain0.reshape(1, C),
        gain1.reshape(1, C),
        flip(first),
        flip(second),
        jnp.swapaxes(upsample, 2, 3),
    )


def solution(mesh):
    in_specs = (
        P("tm", "rows", None, None),
        P(None, "rows", None, None),
        P(None, "rows", None, None),
        P(),
        P(),
        P(None, None, None, None, "rows"),
        P(None, None, None, None, "rows"),
        P(),
    )
    out_specs = P("tm", "rows", None, None)
    return jax.shard_map(shards, mesh=mesh, in_specs=in_specs, out_specs=out_specs, check_vma=False)
```

```python
import jax
import jax.numpy as jnp
from jax import lax
from jax.experimental import pallas as pl
from jax.experimental.pallas import tpu as pltpu
from jax.sharding import PartitionSpec as P

BF = jnp.bfloat16
F32 = jnp.float32
NT = (((1,), (1,)), ((), ()))
W = 160
C = 384
CO = 192
ND = (21, 25)
NQ = (5, 4)
NC = 41
NB = 9
CUTS = ((12, 0), (9, 7))
TAPS = (((0,), (1, 2)), ((0, 1), (2,)))


def mod(a, n):
    return lax.rem(a + n, n)


def kernel(
    frames,
    cache0,
    cache1,
    gain0,
    gain1,
    win0,
    win1,
    up,
    out,
    zb0,
    zb1,
    w0,
    w1,
    xs0,
    xs1,
    bs,
    acc,
    cw,
    ph,
    il,
    ssem,
    rsem,
):
    tm = lax.axis_index("tm")
    r = lax.axis_index("rows")
    x, c = tm // 2, tm % 2
    y, z = r // 8, r % 8
    zdev = lambda d: (tm, y * 8 + mod(z + d, 8))
    ydev = lambda d: (tm, mod(y + d, 4) * 8 + z)
    xdev = lambda d: (mod(x + d, 4) * 2 + c, r)
    tdev = lambda d: (mod(tm + d, 8), r)
    rdev = lambda d: (tm, mod(r + d, 32))
    pair = (x * 2 + 1 - c, r)

    index = {}
    sends = []

    def copy(key, src, dst, dev):
        n = index.setdefault(key, len(index))
        return pltpu.make_async_remote_copy(
            src_ref=src,
            dst_ref=dst,
            send_sem=ssem.at[n],
            recv_sem=rsem.at[n],
            device_id=dev,
            device_id_type=pl.DeviceIdType.MESH,
        )

    def send(key, src, dev, dst=None, when=None):
        dst = src if dst is None else dst

        def go():
            copy(key, src, dst, dev).start()

        if when is None:
            go()
        else:
            pl.when(when)(go)
        sends.append((key, src, dst, dev, when))

    def recv(key, dst, when=None):
        def go():
            copy(key, dst, dst, pair).wait_recv()

        if when is None:
            go()
        else:
            pl.when(when)(go)

    zbs, ws, wins, xss = (zb0, zb1), (w0, w1), (win0, win1), (xs0, xs1)
    caches, gains = (cache0, cache1), (gain0, gain1)

    chunks = []
    for d, q, (nc, ne) in zip(ND, NQ, CUTS):
        chunks.append(
            {
                "b": (0, NB),
                "c": (NB, nc),
                "e": (NB + nc, ne),
                "r": (NB, nc + ne),
                "q": (d, q),
            }
        )

    def unit(v, n):
        local = jnp.where(n < ND[v], n, n + NQ[v] * x)
        second = jnp.where(
            local < 18,
            45 + local,
            jnp.where(
                local < 21,
                23 + local,
                jnp.where(local == 21, 44, jnp.where(local == 40, 40, 41 + local)),
            ),
        )
        return jnp.where(c == 0, local, second)

    def prepare(v):
        zb, win = zbs[v], wins[v]
        zb[z] = jnp.zeros((ND[v] + NQ[v], 16, 128), BF)

        def body(n, _):
            u = unit(v, n)
            lane = pl.multiple_of((u % 3) * 128, 128)
            zb[z, n, 0:12, :] = win[u // 3, :, pl.ds(lane, 128)]
            return 0

        lax.fori_loop(0, ND[v] + NQ[v], body, 0)

    def split(v, g, part):
        lo, n = chunks[v][g]
        cut = (n + 1) // 2
        return ((lo, n), (lo, cut), (lo + cut, n - cut))[part]

    def zview(v, g, d, part=0):
        return zbs[v].at[mod(z + d, 8), pl.ds(*split(v, g, part))]

    def zstart(v, g):
        for d in (2, -2, 1, -1):
            send(("z", v, g, d), zview(v, g, 0), zdev(d))

    def zpass(v, g):
        for d in (2, -2):
            part = 1 if d > 0 else 2
            recv(("z", v, g, d), zview(v, g, -d))
            send(("z", v, g, 2 * d), zview(v, g, -d, part), zdev(d))
            send(("z", v, g, 3 * d // 2), zview(v, g, -d), zdev(d // 2))

    def zwait(v, g):
        for d in (1, -1, 3, -3):
            recv(("z", v, g, d), zview(v, g, -d))
        for d in (4, -4):
            recv(("z", v, g, d), zview(v, g, -d, 1 if d > 0 else 2))

    row = lax.broadcasted_iota(jnp.int32, (96, 128), 0)
    col = lax.broadcasted_iota(jnp.int32, (96, 128), 1)
    squeeze = jnp.where(row + 4 * (row // 12) == col, 1.0, 0.0).astype(BF)
    ybase = lambda d: pl.multiple_of(mod(y + d, 4) * 96, 96)
    qbase = lambda v, core, d: 41 * core + ND[v] + NQ[v] * mod(x + d, 4)

    def base(v, g, core, d=0):
        return qbase(v, core, d) if g == "q" else 41 * core + chunks[v][g][0]

    def assemble(v, g):
        lo, count = chunks[v][g]
        blocks = [zbs[v][:, lo + n].reshape(128, 128) for n in range(count)]
        rows = jnp.dot(
            squeeze, jnp.concatenate(blocks, axis=1), preferred_element_type=F32
        ).astype(BF)
        first = base(v, g, c)
        for n in range(count):
            ws[v][first + n, pl.ds(ybase(0), 96), :] = rows[:, 128 * n : 128 * n + 128]

    def yview(v, g, d, part, core=None):
        lo, n = split(v, g, part)
        lo = lo - chunks[v][g][0]
        first = base(v, g, c if core is None else core) + lo
        return ws[v].at[pl.ds(first, n), pl.ds(ybase(d), 96), :]

    def ystart(v, g):
        send(("yf1", v, g), yview(v, g, 0, 0), ydev(1))
        send(("yb1", v, g), yview(v, g, 0, 0), ydev(-1))
        yhand(v, g, 0)

    def ypass(v, g):
        recv(("yf1", v, g), yview(v, g, -1, 0))
        send(("yf2", v, g), yview(v, g, -1, 1), ydev(1), when=z != 0)
        recv(("yb1", v, g), yview(v, g, 1, 0))
        send(("yb2", v, g), yview(v, g, 1, 2), ydev(-1), when=z != 7)
        yhand(v, g, -1)
        yhand(v, g, 1)

    def ywait(v, g):
        recv(("yf2", v, g), yview(v, g, -2, 1), z != 0)
        send(("ye1", v, g), yview(v, g, -2, 1), zdev(-1), when=z == 1)
        recv(("yb2", v, g), yview(v, g, 2, 2), z != 7)
        send(("ye2", v, g), yview(v, g, 2, 2), zdev(1), when=z == 6)
        recv(("ye1", v, g), yview(v, g, -2, 1), z == 0)
        recv(("ye2", v, g), yview(v, g, 2, 2), z == 7)
        yhand(v, g, 2)

    def yhand(v, g, d):
        if g != "q":
            send(("h", v, g, d), yview(v, g, d, 0), pair)

    def xview(v, d, part):
        lo, n = ((0, 1), (1, NQ[v] - 1))[part - 1]
        return ws[v].at[pl.ds(qbase(v, c, d) + lo, n)]

    def xstart(v):
        for first in (1, 2):
            send(("xf", v, first), xview(v, 0, first), xdev(1))
            send(("xb", v, 3 - first), xview(v, 0, 3 - first), xdev(-1))

    def xpass(v, d):
        key, part = ("xf", 1) if d > 0 else ("xb", 2)
        recv((key, v, part), xview(v, -d, part))
        send((key, v, 3), xview(v, -d, part), xdev(d))

    def xsides(v):
        recv(("xf", v, 2), xview(v, -1, 2))
        recv(("xb", v, 1), xview(v, 1, 1))

    def xwait(v):
        recv(("xf", v, 3), xview(v, -2, 1))
        recv(("xb", v, 3), xview(v, 2, 2))

    def cview(v, core, d):
        return ws[v].at[pl.ds(qbase(v, core, d), NQ[v])]

    def hand(v, g, d):
        send(("c", v, g, d), cview(v, c, d), pair)

    def taken(v, g):
        for d in (0, -1, 1, 2):
            recv(("h", v, g, d), yview(v, g, d, 0, 1 - c))

    def alltaken(v):
        for d in (0, 1, -1, 2):
            recv(("c", v, "q", d), cview(v, 1 - c, d))

    def normed(v, values):
        scale = lax.rsqrt(jnp.mean(values * values, axis=-1, keepdims=True) + 1e-06)
        return jax.nn.silu(values * scale * gains[v][...].reshape(1, C)).astype(BF)

    inner_lo, inner_hi, later, first = r > 0, r < 31, tm < 7, tm == 0

    def halo_row(v):
        xs = xss[v]
        own = xs.at[1, 1, pl.ds(2, 2)]
        send(("t1", v), own, tdev(1), xs.at[1, 1, pl.ds(0, 2)], later)

    def halo_start(v):
        xs = xss[v]
        own = xs.at[1, 1, pl.ds(2, 2)]
        send(("up", v), own, rdev(1), xs.at[1, 0, pl.ds(2, 2)], inner_hi)
        send(("dn", v), own, rdev(-1), xs.at[1, 2, pl.ds(2, 2)], inner_lo)
        away = later & (c == 1)
        below, above = (mod(tm + 1, 8), mod(r + 1, 32)), (mod(tm + 1, 8), mod(r - 1, 32))
        send(("t0", v), own, below, xs.at[1, 0, pl.ds(0, 2)], away & inner_hi)
        send(("t2", v), own, above, xs.at[1, 2, pl.ds(0, 2)], away & inner_lo)

    def cache_start(v):
        xs = xss[v]

        @pl.when(first)
        def _():
            xs[1, 1, 0:2] = caches[v][...]

        old = xs.at[1, 1, pl.ds(0, 2)]
        send(("cu", v), old, rdev(1), xs.at[1, 0, pl.ds(0, 2)], first & inner_hi)
        send(("cn", v), old, rdev(-1), xs.at[1, 2, pl.ds(0, 2)], first & inner_lo)

        @pl.when(r == 0)
        def _():
            xs[1, 0] = jnp.zeros((4, W, C), BF)

        @pl.when(r == 31)
        def _():
            xs[1, 2] = jnp.zeros((4, W, C), BF)

    def halo_pass(v):
        xs = xss[v]
        low, high = xs.at[1, 0, pl.ds(2, 2)], xs.at[1, 2, pl.ds(2, 2)]
        recv(("up", v), low, inner_lo)
        send(("t0", v), low, tdev(1), xs.at[1, 0, pl.ds(0, 2)], (c == 0) & inner_lo)
        recv(("dn", v), high, inner_hi)
        send(("t2", v), high, tdev(1), xs.at[1, 2, pl.ds(0, 2)], (c == 0) & inner_hi)

    def halo_wait(v):
        xs = xss[v]
        old = [xs.at[1, j, pl.ds(0, 2)] for j in range(3)]
        recv(("t1", v), old[1], tm > 0)
        recv(("t0", v), old[0], (tm > 0) & inner_lo)
        recv(("t2", v), old[2], (tm > 0) & inner_hi)
        recv(("cu", v), old[0], first & inner_lo)
        recv(("cn", v), old[2], first & inner_hi)

    def shift(buf, j, f):
        v = buf[1, j, f].astype(F32)
        at = lax.broadcasted_iota(jnp.int32, v.shape, 0)
        buf[0, j, f] = jnp.where(at == 0, 0.0, pltpu.roll(v, 1, 0)).astype(BF)
        buf[2, j, f] = jnp.where(at == W - 1, 0.0, pltpu.roll(v, W - 1, 0)).astype(BF)

    def shifts(buf, js, f0, n):
        for j in js:

            def body(f, _):
                shift(buf, j, f0 + f)
                return 0

            lax.fori_loop(0, n, body, 0)

    def conv(v, *pieces):
        xs, w = xss[v], ws[v]

        def body(n, _):
            ij = jnp.int32(pieces[0])
            for m in range(1, len(pieces)):
                ij = jnp.where(n == m, pieces[m], ij)
            i, j = ij // 3, ij % 3
            low = 9 * ij - jnp.where((ij == 5) | (ij == 6), 4, 0)
            high = low + jnp.where(ij == 4, 18, 0)
            lhs = jnp.concatenate(
                [xs[k, j, pl.ds(i, 2)].reshape(2 * W, C) for k in range(3)], axis=1
            )
            rhs = jnp.concatenate([w[(low if u < 5 else high) + u] for u in range(9)], axis=1)
            acc[...] += lax.dot_general(lhs, rhs, NT, preferred_element_type=F32)
            return 0

        lax.fori_loop(0, len(pieces), body, 0)

    def combine():
        for a in range(2):
            for p in range(2):
                for b in range(2):
                    for q in range(2):
                        total = sum(
                            up[j, k].astype(F32) for j in TAPS[a][p] for k in TAPS[b][q]
                        )
                        cw[a, p, b, q] = total.astype(BF)

    def phase(a, b, p):
        lhs = jnp.concatenate(
            [bs[b + q, a + p].reshape(2 * W, C) for q in range(2)], axis=1
        )
        rhs = jnp.concatenate([cw[a, p, b, q] for q in range(2)], axis=1)
        return lax.dot_general(lhs, rhs, NT, preferred_element_type=F32)

    barrier = pltpu.get_barrier_semaphore()
    near = [f(d) for f in (zdev, ydev, xdev, tdev, rdev) for d in (1, -1)]
    near += [zdev(2), zdev(-2)]
    near += [(mod(tm + d, 8), mod(r + e, 32)) for d in (1, -1) for e in (1, -1)]
    for dev in near:
        pl.semaphore_signal(barrier, inc=1, device_id=dev, device_id_type=pl.DeviceIdType.MESH)
    prepare(0)
    pl.semaphore_wait(barrier, len(near))

    zstart(0, "q")
    xs0[1, 1, 2:4] = normed(0, frames[...].astype(F32).reshape(2 * W, C)).reshape(2, W, C)
    halo_row(0)
    zpass(0, "q")
    zstart(0, "b")
    zstart(0, "c")
    zwait(0, "q")
    assemble(0, "q")
    ystart(0, "q")
    zpass(0, "b")
    prepare(1)
    zpass(0, "c")
    zwait(0, "b")
    assemble(0, "b")
    ypass(0, "q")
    ystart(0, "b")
    zwait(0, "c")
    assemble(0, "c")
    ystart(0, "c")
    ywait(0, "q")
    xstart(0)
    hand(0, "q", 0)
    zstart(1, "q")
    zstart(1, "b")
    halo_start(0)
    cache_start(0)
    zstart(1, "r")
    ypass(0, "b")
    xpass(0, 1)
    zpass(1, "q")
    zpass(1, "b")
    shifts(xs0, (1,), 2, 2)
    ypass(0, "c")
    zwait(1, "q")
    assemble(1, "q")
    ystart(1, "q")
    xpass(0, -1)
    ywait(0, "b")
    halo_pass(0)
    zwait(1, "b")
    assemble(1, "b")
    ystart(1, "b")
    ywait(0, "c")
    xsides(0)
    hand(0, "q", 1)
    hand(0, "q", -1)
    zpass(1, "r")
    ypass(1, "q")
    acc[...] = jnp.zeros_like(acc)
    halo_wait(0)
    shifts(xs0, (0, 2), 2, 2)
    shifts(xs0, (0, 1, 2), 0, 2)
    taken(0, "b")
    conv(0, 0, 5)
    xwait(0)
    hand(0, "q", 2)
    ywait(1, "q")
    xstart(1)
    hand(1, "q", 0)
    taken(0, "c")
    conv(0, 1, 6)
    zwait(1, "r")
    assemble(1, "c")
    ystart(1, "c")
    assemble(1, "e")
    ystart(1, "e")
    ypass(1, "b")
    alltaken(0)
    conv(0, 2, 3, 4, 7, 8)
    xs1[1, 1, 2:4] = normed(1, acc[...].astype(BF).astype(F32)).reshape(2, W, C)
    halo_row(1)
    halo_start(1)
    cache_start(1)
    xpass(1, 1)
    acc[...] = frames[...].astype(F32).reshape(2 * W, C)
    shifts(xs1, (1,), 2, 2)
    xpass(1, -1)
    ypass(1, "c")
    combine()
    ywait(1, "b")
    xsides(1)
    hand(1, "q", 1)
    hand(1, "q", -1)
    halo_pass(1)
    ypass(1, "e")
    xwait(1)
    hand(1, "q", 2)
    ywait(1, "c")
    halo_wait(1)
    shifts(xs1, (0, 2), 2, 2)
    shifts(xs1, (0, 1, 2), 0, 2)
    taken(1, "b")
    conv(1, 0, 5)
    ywait(1, "e")
    taken(1, "c")
    conv(1, 1, 6)
    alltaken(1)
    conv(1, 3, 8)
    taken(1, "e")
    conv(1, 2, 4, 7)

    bs[1, 1] = acc[...].astype(BF).reshape(2, W, C)
    send("bu", bs.at[1, 1], rdev(1), bs.at[1, 0], inner_hi)
    send("bd", bs.at[1, 1], rdev(-1), bs.at[1, 2], inner_lo)

    @pl.when(r == 0)
    def _():
        bs[1, 0] = jnp.zeros((2, W, C), BF)

    @pl.when(r == 31)
    def _():
        bs[1, 2] = jnp.zeros((2, W, C), BF)

    shifts(bs, (1,), 0, 2)
    for a in range(2):
        for b in range(2):
            ph[a, b] = phase(a, b, 1 - a)
    recv("bu", bs.at[1, 0], inner_lo)
    recv("bd", bs.at[1, 2], inner_hi)
    shifts(bs, (0, 2), 0, 2)
    for a in range(2):
        for b in range(2):
            total = ph[a, b] + phase(a, b, a)
            for f in range(2):
                part = total[f * W : (f + 1) * W]
                il[f, pl.ds(b, W, stride=2), :] = part[:, :128]
                il[2 + f, pl.ds(b, W, stride=2), 0:64] = part[:, 128:]
        for f in range(2):
            out[f, a, :, 0:128] = il[f].astype(BF)
            out[f, a, :, 128:192] = il[2 + f, :, 0:64].astype(BF)

    for key, src, dst, dev, when in sends:
        done = lambda k=key, s=src, d=dst, e=dev: copy(k, s, d, e).wait_send()
        if when is None:
            done()
        else:
            pl.when(when)(done)


def shards(frames, cache0, cache1, gain0, gain1, first, second, upsample):
    vmem = pl.BlockSpec(memory_space=pltpu.VMEM)
    block = lambda v: v.reshape(2, W, C)
    flip = lambda v: jnp.swapaxes(v, 3, 4).reshape(27, 12, C)
    return pl.pallas_call(
        kernel,
        out_shape=jax.ShapeDtypeStruct((2, 2, 2 * W, CO), BF),
        in_specs=[vmem] * 8,
        out_specs=vmem,
        scratch_shapes=[
            pltpu.VMEM((8, ND[0] + NQ[0], 16, 128), BF),
            pltpu.VMEM((8, ND[1] + NQ[1], 16, 128), BF),
            pltpu.VMEM((2 * NC, C, 128), BF),
            pltpu.VMEM((2 * NC, C, 128), BF),
            pltpu.VMEM((3, 3, 4, W, C), BF),
            pltpu.VMEM((3, 3, 4, W, C), BF),
            pltpu.VMEM((3, 3, 2, W, C), BF),
            pltpu.VMEM((2 * W, C), F32),
            pltpu.VMEM((2, 2, 2, 2, CO, C), BF),
            pltpu.VMEM((2, 2, 2 * W, CO), F32),
            pltpu.VMEM((4, 2 * W, 128), F32),
            pltpu.SemaphoreType.DMA((176,)),
            pltpu.SemaphoreType.DMA((176,)),
        ],
        compiler_params=pltpu.CompilerParams(
            collective_id=0, has_side_effects=True, vmem_limit_bytes=60 << 20
        ),
    )(
        block(frames),
        block(cache0),
        block(cache1),
        gain0,
        gain1,
        flip(first),
        flip(second),
        jnp.swapaxes(upsample, 2, 3),
    )


def solution(mesh):
    in_specs = (
        P("tm", "rows", None, None),
        P(None, "rows", None, None),
        P(None, "rows", None, None),
        P(),
        P(),
        P(None, None, None, None, "rows"),
        P(None, None, None, None, "rows"),
        P(),
    )
    out_specs = P("tm", "rows", None, None)
    return jax.shard_map(shards, mesh=mesh, in_specs=in_specs, out_specs=out_specs, check_vma=False)
```

```python
import jax
import jax.numpy as jnp
from jax import lax
from jax.experimental import pallas as pl
from jax.experimental.pallas import tpu as pltpu
from jax.sharding import PartitionSpec as P

BF = jnp.bfloat16
F32 = jnp.float32
NT = (((1,), (1,)), ((), ()))
W = 160
C = 384
CO = 192
ND = (21, 25)
NQ = (5, 4)
NC = 41
NB = 9
CUTS = ((12, 0), (9, 7))
TAPS = (((0,), (1, 2)), ((0, 1), (2,)))


def mod(a, n):
    return lax.rem(a + n, n)


def kernel(
    frames,
    cache0,
    cache1,
    gain0,
    gain1,
    win0,
    win1,
    up,
    out,
    zb0,
    zb1,
    w0,
    w1,
    xs0,
    xs1,
    bs,
    acc,
    cw,
    ph,
    il,
    ssem,
    rsem,
):
    tm = lax.axis_index("tm")
    r = lax.axis_index("rows")
    x, c = tm // 2, tm % 2
    y, z = r // 8, r % 8
    zdev = lambda d: (tm, y * 8 + mod(z + d, 8))
    ydev = lambda d: (tm, mod(y + d, 4) * 8 + z)
    xdev = lambda d: (mod(x + d, 4) * 2 + c, r)
    tdev = lambda d: (mod(tm + d, 8), r)
    rdev = lambda d: (tm, mod(r + d, 32))
    pair = (x * 2 + 1 - c, r)

    index = {}
    sends = []

    def copy(key, src, dst, dev):
        n = index.setdefault(key, len(index))
        return pltpu.make_async_remote_copy(
            src_ref=src,
            dst_ref=dst,
            send_sem=ssem.at[n],
            recv_sem=rsem.at[n],
            device_id=dev,
            device_id_type=pl.DeviceIdType.MESH,
        )

    def send(key, src, dev, dst=None, when=None):
        dst = src if dst is None else dst

        def go():
            copy(key, src, dst, dev).start()

        if when is None:
            go()
        else:
            pl.when(when)(go)
        sends.append((key, src, dst, dev, when))

    def recv(key, dst, when=None):
        def go():
            copy(key, dst, dst, pair).wait_recv()

        if when is None:
            go()
        else:
            pl.when(when)(go)

    zbs, ws, wins, xss = (zb0, zb1), (w0, w1), (win0, win1), (xs0, xs1)
    caches, gains = (cache0, cache1), (gain0, gain1)

    chunks = []
    for d, q, (nc, ne) in zip(ND, NQ, CUTS):
        chunks.append(
            {
                "b": (0, NB),
                "c": (NB, nc),
                "e": (NB + nc, ne),
                "r": (NB, nc + ne),
                "q": (d, q),
            }
        )

    def unit(v, n):
        local = jnp.where(n < ND[v], n, n + NQ[v] * x)
        second = jnp.where(
            local < 18,
            45 + local,
            jnp.where(
                local < 21,
                23 + local,
                jnp.where(local == 21, 44, jnp.where(local == 40, 40, 41 + local)),
            ),
        )
        return jnp.where(c == 0, local, second)

    def prepare(v):
        zb, win = zbs[v], wins[v]
        zb[z] = jnp.zeros((ND[v] + NQ[v], 16, 128), BF)

        def body(n, _):
            u = unit(v, n)
            lane = pl.multiple_of((u % 3) * 128, 128)
            zb[z, n, 0:12, :] = win[u // 3, :, pl.ds(lane, 128)]
            return 0

        lax.fori_loop(0, ND[v] + NQ[v], body, 0)

    def split(v, g, part):
        lo, n = chunks[v][g]
        cut = (n + 1) // 2
        return ((lo, n), (lo, cut), (lo + cut, n - cut))[part]

    def zview(v, g, d, part=0):
        return zbs[v].at[mod(z + d, 8), pl.ds(*split(v, g, part))]

    def zstart(v, g):
        for d in (2, -2, 1, -1):
            send(("z", v, g, d), zview(v, g, 0), zdev(d))

    def zpass(v, g):
        for d in (2, -2):
            part = 1 if d > 0 else 2
            recv(("z", v, g, d), zview(v, g, -d))
            send(("z", v, g, 2 * d), zview(v, g, -d, part), zdev(d))
            send(("z", v, g, 3 * d // 2), zview(v, g, -d), zdev(d // 2))

    def zwait(v, g):
        for d in (1, -1, 3, -3):
            recv(("z", v, g, d), zview(v, g, -d))
        for d in (4, -4):
            recv(("z", v, g, d), zview(v, g, -d, 1 if d > 0 else 2))

    row = lax.broadcasted_iota(jnp.int32, (96, 128), 0)
    col = lax.broadcasted_iota(jnp.int32, (96, 128), 1)
    squeeze = jnp.where(row + 4 * (row // 12) == col, 1.0, 0.0).astype(BF)
    ybase = lambda d: pl.multiple_of(mod(y + d, 4) * 96, 96)
    qbase = lambda v, core, d: 41 * core + ND[v] + NQ[v] * mod(x + d, 4)

    def base(v, g, core, d=0):
        return qbase(v, core, d) if g == "q" else 41 * core + chunks[v][g][0]

    def assemble(v, g):
        lo, count = chunks[v][g]
        blocks = [zbs[v][:, lo + n].reshape(128, 128) for n in range(count)]
        rows = jnp.dot(
            squeeze, jnp.concatenate(blocks, axis=1), preferred_element_type=F32
        ).astype(BF)
        first = base(v, g, c)
        for n in range(count):
            ws[v][first + n, pl.ds(ybase(0), 96), :] = rows[:, 128 * n : 128 * n + 128]

    def yview(v, g, d, part, core=None):
        lo, n = split(v, g, part)
        lo = lo - chunks[v][g][0]
        first = base(v, g, c if core is None else core) + lo
        return ws[v].at[pl.ds(first, n), pl.ds(ybase(d), 96), :]

    def ystart(v, g):
        send(("yf1", v, g), yview(v, g, 0, 0), ydev(1))
        send(("yb1", v, g), yview(v, g, 0, 0), ydev(-1))
        yhand(v, g, 0)

    def ypass(v, g):
        recv(("yf1", v, g), yview(v, g, -1, 0))
        send(("yf2", v, g), yview(v, g, -1, 1), ydev(1), when=z != 0)
        recv(("yb1", v, g), yview(v, g, 1, 0))
        send(("yb2", v, g), yview(v, g, 1, 2), ydev(-1), when=z != 7)
        yhand(v, g, -1)
        yhand(v, g, 1)

    def ywait(v, g):
        recv(("yf2", v, g), yview(v, g, -2, 1), z != 0)
        send(("ye1", v, g), yview(v, g, -2, 1), zdev(-1), when=z == 1)
        recv(("yb2", v, g), yview(v, g, 2, 2), z != 7)
        send(("ye2", v, g), yview(v, g, 2, 2), zdev(1), when=z == 6)
        recv(("ye1", v, g), yview(v, g, -2, 1), z == 0)
        recv(("ye2", v, g), yview(v, g, 2, 2), z == 7)
        yhand(v, g, 2)

    def yhand(v, g, d):
        if g != "q":
            send(("h", v, g, d), yview(v, g, d, 0), pair)

    def xview(v, d, part):
        lo, n = ((0, 1), (1, NQ[v] - 1))[part - 1]
        return ws[v].at[pl.ds(qbase(v, c, d) + lo, n)]

    def xstart(v):
        for first in (1, 2):
            send(("xf", v, first), xview(v, 0, first), xdev(1))
            send(("xb", v, 3 - first), xview(v, 0, 3 - first), xdev(-1))

    def xpass(v, d):
        key, part = ("xf", 1) if d > 0 else ("xb", 2)
        recv((key, v, part), xview(v, -d, part))
        send((key, v, 3), xview(v, -d, part), xdev(d))

    def xsides(v):
        recv(("xf", v, 2), xview(v, -1, 2))
        recv(("xb", v, 1), xview(v, 1, 1))

    def xwait(v):
        recv(("xf", v, 3), xview(v, -2, 1))
        recv(("xb", v, 3), xview(v, 2, 2))

    def cview(v, core, d):
        return ws[v].at[pl.ds(qbase(v, core, d), NQ[v])]

    def hand(v, g, d):
        send(("c", v, g, d), cview(v, c, d), pair)

    def taken(v, g):
        for d in (0, -1, 1, 2):
            recv(("h", v, g, d), yview(v, g, d, 0, 1 - c))

    def alltaken(v):
        for d in (0, 1, -1, 2):
            recv(("c", v, "q", d), cview(v, 1 - c, d))

    def normed(v, values):
        scale = lax.rsqrt(jnp.mean(values * values, axis=-1, keepdims=True) + 1e-06)
        return jax.nn.silu(values * scale * gains[v][...].reshape(1, C)).astype(BF)

    inner_lo, inner_hi, later, first = r > 0, r < 31, tm < 7, tm == 0

    def halo_row(v):
        xs = xss[v]
        own = xs.at[1, 1, pl.ds(2, 2)]
        send(("t1", v), own, tdev(1), xs.at[1, 1, pl.ds(0, 2)], later)

    def halo_start(v):
        xs = xss[v]
        own = xs.at[1, 1, pl.ds(2, 2)]
        send(("up", v), own, rdev(1), xs.at[1, 0, pl.ds(2, 2)], inner_hi)
        send(("dn", v), own, rdev(-1), xs.at[1, 2, pl.ds(2, 2)], inner_lo)
        away = later & (c == 1)
        below, above = (mod(tm + 1, 8), mod(r + 1, 32)), (mod(tm + 1, 8), mod(r - 1, 32))
        send(("t0", v), own, below, xs.at[1, 0, pl.ds(0, 2)], away & inner_hi)
        send(("t2", v), own, above, xs.at[1, 2, pl.ds(0, 2)], away & inner_lo)

    def cache_start(v):
        xs = xss[v]

        @pl.when(first)
        def _():
            xs[1, 1, 0:2] = caches[v][...]

        old = xs.at[1, 1, pl.ds(0, 2)]
        send(("cu", v), old, rdev(1), xs.at[1, 0, pl.ds(0, 2)], first & inner_hi)
        send(("cn", v), old, rdev(-1), xs.at[1, 2, pl.ds(0, 2)], first & inner_lo)

        @pl.when(r == 0)
        def _():
            xs[1, 0] = jnp.zeros((4, W, C), BF)

        @pl.when(r == 31)
        def _():
            xs[1, 2] = jnp.zeros((4, W, C), BF)

    def halo_pass(v):
        xs = xss[v]
        low, high = xs.at[1, 0, pl.ds(2, 2)], xs.at[1, 2, pl.ds(2, 2)]
        recv(("up", v), low, inner_lo)
        send(("t0", v), low, tdev(1), xs.at[1, 0, pl.ds(0, 2)], (c == 0) & inner_lo)
        recv(("dn", v), high, inner_hi)
        send(("t2", v), high, tdev(1), xs.at[1, 2, pl.ds(0, 2)], (c == 0) & inner_hi)

    def halo_wait(v):
        xs = xss[v]
        old = [xs.at[1, j, pl.ds(0, 2)] for j in range(3)]
        recv(("t1", v), old[1], tm > 0)
        recv(("t0", v), old[0], (tm > 0) & inner_lo)
        recv(("t2", v), old[2], (tm > 0) & inner_hi)
        recv(("cu", v), old[0], first & inner_lo)
        recv(("cn", v), old[2], first & inner_hi)

    def shift(buf, j, f):
        v = buf[1, j, f].astype(F32)
        at = lax.broadcasted_iota(jnp.int32, v.shape, 0)
        buf[0, j, f] = jnp.where(at == 0, 0.0, pltpu.roll(v, 1, 0)).astype(BF)
        buf[2, j, f] = jnp.where(at == W - 1, 0.0, pltpu.roll(v, W - 1, 0)).astype(BF)

    def shifts(buf, js, f0, n):
        for j in js:

            def body(f, _):
                shift(buf, j, f0 + f)
                return 0

            lax.fori_loop(0, n, body, 0)

    def conv(v, *pieces):
        xs, w = xss[v], ws[v]

        def body(n, _):
            ij = jnp.int32(pieces[0])
            for m in range(1, len(pieces)):
                ij = jnp.where(n == m, pieces[m], ij)
            i, j = ij // 3, ij % 3
            low = 9 * ij - jnp.where((ij == 5) | (ij == 6), 4, 0)
            high = low + jnp.where(ij == 4, 18, 0)
            lhs = jnp.concatenate(
                [xs[k, j, pl.ds(i, 2)].reshape(2 * W, C) for k in range(3)], axis=1
            )
            rhs = jnp.concatenate([w[(low if u < 5 else high) + u] for u in range(9)], axis=1)
            acc[...] += lax.dot_general(lhs, rhs, NT, preferred_element_type=F32)
            return 0

        lax.fori_loop(0, len(pieces), body, 0)

    def combine():
        for a in range(2):
            for p in range(2):
                for b in range(2):
                    for q in range(2):
                        total = sum(
                            up[j, k].astype(F32) for j in TAPS[a][p] for k in TAPS[b][q]
                        )
                        cw[a, p, b, q] = total.astype(BF)

    def phase(a, b, p):
        lhs = jnp.concatenate(
            [bs[b + q, a + p].reshape(2 * W, C) for q in range(2)], axis=1
        )
        rhs = jnp.concatenate([cw[a, p, b, q] for q in range(2)], axis=1)
        return lax.dot_general(lhs, rhs, NT, preferred_element_type=F32)

    barrier = pltpu.get_barrier_semaphore()
    near = [f(d) for f in (zdev, ydev, xdev, tdev, rdev) for d in (1, -1)]
    near += [zdev(2), zdev(-2)]
    near += [(mod(tm + d, 8), mod(r + e, 32)) for d in (1, -1) for e in (1, -1)]
    for dev in near:
        pl.semaphore_signal(barrier, inc=1, device_id=dev, device_id_type=pl.DeviceIdType.MESH)
    prepare(0)
    pl.semaphore_wait(barrier, len(near))

    zstart(0, "q")
    xs0[1, 1, 2:4] = normed(0, frames[...].astype(F32).reshape(2 * W, C)).reshape(2, W, C)
    halo_row(0)
    zpass(0, "q")
    zstart(0, "b")
    zstart(0, "c")
    zwait(0, "q")
    assemble(0, "q")
    ystart(0, "q")
    zpass(0, "b")
    prepare(1)
    zpass(0, "c")
    zwait(0, "b")
    assemble(0, "b")
    ypass(0, "q")
    ystart(0, "b")
    zwait(0, "c")
    assemble(0, "c")
    ystart(0, "c")
    ywait(0, "q")
    xstart(0)
    hand(0, "q", 0)
    zstart(1, "q")
    zstart(1, "b")
    halo_start(0)
    cache_start(0)
    zstart(1, "r")
    combine()
    ypass(0, "b")
    xpass(0, 1)
    zpass(1, "q")
    zpass(1, "b")
    shifts(xs0, (1,), 2, 2)
    ypass(0, "c")
    zwait(1, "q")
    assemble(1, "q")
    ystart(1, "q")
    xpass(0, -1)
    ywait(0, "b")
    zwait(1, "b")
    assemble(1, "b")
    ystart(1, "b")
    halo_pass(0)
    zpass(1, "r")
    ywait(0, "c")
    xsides(0)
    hand(0, "q", 1)
    hand(0, "q", -1)
    ypass(1, "q")
    zwait(1, "r")
    assemble(1, "c")
    ystart(1, "c")
    assemble(1, "e")
    ystart(1, "e")
    acc[...] = jnp.zeros_like(acc)
    halo_wait(0)
    shifts(xs0, (0, 2), 2, 2)
    shifts(xs0, (0, 1, 2), 0, 2)
    taken(0, "b")
    conv(0, 0, 5)
    xwait(0)
    hand(0, "q", 2)
    ypass(1, "b")
    ywait(1, "q")
    xstart(1)
    hand(1, "q", 0)
    taken(0, "c")
    conv(0, 1, 6)
    alltaken(0)
    conv(0, 2, 3, 4, 7, 8)
    xs1[1, 1, 2:4] = normed(1, acc[...].astype(BF).astype(F32)).reshape(2, W, C)
    halo_row(1)
    halo_start(1)
    cache_start(1)
    ypass(1, "c")
    xpass(1, 1)
    acc[...] = frames[...].astype(F32).reshape(2 * W, C)
    shifts(xs1, (1,), 2, 2)
    ypass(1, "e")
    xpass(1, -1)
    ywait(1, "b")
    xsides(1)
    hand(1, "q", 1)
    hand(1, "q", -1)
    halo_pass(1)
    ywait(1, "c")
    ywait(1, "e")
    xwait(1)
    hand(1, "q", 2)
    halo_wait(1)
    shifts(xs1, (0, 2), 2, 2)
    shifts(xs1, (0, 1, 2), 0, 2)
    taken(1, "b")
    conv(1, 0, 5)
    taken(1, "c")
    conv(1, 1, 6)
    alltaken(1)
    taken(1, "e")
    conv(1, 2, 3, 4, 7, 8)

    bs[1, 1] = acc[...].astype(BF).reshape(2, W, C)
    send("bu", bs.at[1, 1], rdev(1), bs.at[1, 0], inner_hi)
    send("bd", bs.at[1, 1], rdev(-1), bs.at[1, 2], inner_lo)

    @pl.when(r == 0)
    def _():
        bs[1, 0] = jnp.zeros((2, W, C), BF)

    @pl.when(r == 31)
    def _():
        bs[1, 2] = jnp.zeros((2, W, C), BF)

    shifts(bs, (1,), 0, 2)
    for a in range(2):
        for b in range(2):
            ph[a, b] = phase(a, b, 1 - a)
    recv("bu", bs.at[1, 0], inner_lo)
    recv("bd", bs.at[1, 2], inner_hi)
    shifts(bs, (0, 2), 0, 2)
    for a in range(2):
        for b in range(2):
            total = ph[a, b] + phase(a, b, a)
            for f in range(2):
                part = total[f * W : (f + 1) * W]
                il[f, pl.ds(b, W, stride=2), :] = part[:, :128]
                il[2 + f, pl.ds(b, W, stride=2), 0:64] = part[:, 128:]
        for f in range(2):
            out[f, a, :, 0:128] = il[f].astype(BF)
            out[f, a, :, 128:192] = il[2 + f, :, 0:64].astype(BF)

    for key, src, dst, dev, when in sends:
        done = lambda k=key, s=src, d=dst, e=dev: copy(k, s, d, e).wait_send()
        if when is None:
            done()
        else:
            pl.when(when)(done)


def shards(frames, cache0, cache1, gain0, gain1, first, second, upsample):
    vmem = pl.BlockSpec(memory_space=pltpu.VMEM)
    block = lambda v: v.reshape(2, W, C)
    flip = lambda v: jnp.swapaxes(v, 3, 4).reshape(27, 12, C)
    return pl.pallas_call(
        kernel,
        out_shape=jax.ShapeDtypeStruct((2, 2, 2 * W, CO), BF),
        in_specs=[vmem] * 8,
        out_specs=vmem,
        scratch_shapes=[
            pltpu.VMEM((8, ND[0] + NQ[0], 16, 128), BF),
            pltpu.VMEM((8, ND[1] + NQ[1], 16, 128), BF),
            pltpu.VMEM((2 * NC, C, 128), BF),
            pltpu.VMEM((2 * NC, C, 128), BF),
            pltpu.VMEM((3, 3, 4, W, C), BF),
            pltpu.VMEM((3, 3, 4, W, C), BF),
            pltpu.VMEM((3, 3, 2, W, C), BF),
            pltpu.VMEM((2 * W, C), F32),
            pltpu.VMEM((2, 2, 2, 2, CO, C), BF),
            pltpu.VMEM((2, 2, 2 * W, CO), F32),
            pltpu.VMEM((4, 2 * W, 128), F32),
            pltpu.SemaphoreType.DMA((176,)),
            pltpu.SemaphoreType.DMA((176,)),
        ],
        compiler_params=pltpu.CompilerParams(
            collective_id=0, has_side_effects=True, vmem_limit_bytes=60 << 20
        ),
    )(
        block(frames),
        block(cache0),
        block(cache1),
        gain0,
        gain1,
        flip(first),
        flip(second),
        jnp.swapaxes(upsample, 2, 3),
    )


def solution(mesh):
    in_specs = (
        P("tm", "rows", None, None),
        P(None, "rows", None, None),
        P(None, "rows", None, None),
        P(),
        P(),
        P(None, None, None, None, "rows"),
        P(None, None, None, None, "rows"),
        P(),
    )
    out_specs = P("tm", "rows", None, None)
    return jax.shard_map(shards, mesh=mesh, in_specs=in_specs, out_specs=out_specs, check_vma=False)
```

```python
import jax
import jax.numpy as jnp
from jax import lax
from jax.experimental import pallas as pl
from jax.experimental.pallas import tpu as pltpu
from jax.sharding import PartitionSpec as P

BF = jnp.bfloat16
F32 = jnp.float32
NT = (((1,), (1,)), ((), ()))
W = 160
C = 384
CO = 192
ND = (21, 25)
NQ = (5, 4)
NC = 41
NB = 9
CUTS = ((12, 0), (9, 7))
TAPS = (((0,), (1, 2)), ((0, 1), (2,)))


def mod(a, n):
    return lax.rem(a + n, n)


def kernel(
    frames,
    cache0,
    cache1,
    gain0,
    gain1,
    win0,
    win1,
    up,
    out,
    zb0,
    zb1,
    w0,
    w1,
    xs0,
    xs1,
    bs,
    acc,
    cw,
    ph,
    il,
    ssem,
    rsem,
):
    tm = lax.axis_index("tm")
    r = lax.axis_index("rows")
    x, c = tm // 2, tm % 2
    y, z = r // 8, r % 8
    zdev = lambda d: (tm, y * 8 + mod(z + d, 8))
    ydev = lambda d: (tm, mod(y + d, 4) * 8 + z)
    xdev = lambda d: (mod(x + d, 4) * 2 + c, r)
    tdev = lambda d: (mod(tm + d, 8), r)
    rdev = lambda d: (tm, mod(r + d, 32))
    pair = (x * 2 + 1 - c, r)

    index = {}
    sends = []

    def copy(key, src, dst, dev):
        n = index.setdefault(key, len(index))
        return pltpu.make_async_remote_copy(
            src_ref=src,
            dst_ref=dst,
            send_sem=ssem.at[n],
            recv_sem=rsem.at[n],
            device_id=dev,
            device_id_type=pl.DeviceIdType.MESH,
        )

    def send(key, src, dev, dst=None, when=None):
        dst = src if dst is None else dst

        def go():
            copy(key, src, dst, dev).start()

        if when is None:
            go()
        else:
            pl.when(when)(go)
        sends.append((key, src, dst, dev, when))

    def recv(key, dst, when=None):
        def go():
            copy(key, dst, dst, pair).wait_recv()

        if when is None:
            go()
        else:
            pl.when(when)(go)

    zbs, ws, wins, xss = (zb0, zb1), (w0, w1), (win0, win1), (xs0, xs1)
    caches, gains = (cache0, cache1), (gain0, gain1)

    chunks = []
    for d, q, (nc, ne) in zip(ND, NQ, CUTS):
        chunks.append(
            {
                "b": (0, NB),
                "c": (NB, nc),
                "e": (NB + nc, ne),
                "r": (NB, nc + ne),
                "q": (d, q),
            }
        )

    def unit(v, n):
        local = jnp.where(n < ND[v], n, n + NQ[v] * x)
        second = jnp.where(
            local < 18,
            45 + local,
            jnp.where(
                local < 21,
                23 + local,
                jnp.where(local == 21, 44, jnp.where(local == 40, 40, 41 + local)),
            ),
        )
        return jnp.where(c == 0, local, second)

    def prepare(v):
        zb, win = zbs[v], wins[v]
        zb[z] = jnp.zeros((ND[v] + NQ[v], 16, 128), BF)

        def body(n, _):
            u = unit(v, n)
            lane = pl.multiple_of((u % 3) * 128, 128)
            zb[z, n, 0:12, :] = win[u // 3, :, pl.ds(lane, 128)]
            return 0

        lax.fori_loop(0, ND[v] + NQ[v], body, 0)

    def split(v, g, part):
        lo, n = chunks[v][g]
        cut = (n + 1) // 2
        return ((lo, n), (lo, cut), (lo + cut, n - cut))[part]

    def zview(v, g, d, part=0):
        return zbs[v].at[mod(z + d, 8), pl.ds(*split(v, g, part))]

    def zstart(v, g):
        for d in (2, -2, 1, -1):
            send(("z", v, g, d), zview(v, g, 0), zdev(d))

    def zpass(v, g):
        for d in (2, -2):
            part = 1 if d > 0 else 2
            recv(("z", v, g, d), zview(v, g, -d))
            send(("z", v, g, 2 * d), zview(v, g, -d, part), zdev(d))
            send(("z", v, g, 3 * d // 2), zview(v, g, -d), zdev(d // 2))

    def zwait(v, g):
        for d in (1, -1, 3, -3):
            recv(("z", v, g, d), zview(v, g, -d))
        for d in (4, -4):
            recv(("z", v, g, d), zview(v, g, -d, 1 if d > 0 else 2))

    row = lax.broadcasted_iota(jnp.int32, (96, 128), 0)
    col = lax.broadcasted_iota(jnp.int32, (96, 128), 1)
    squeeze = jnp.where(row + 4 * (row // 12) == col, 1.0, 0.0).astype(BF)
    ybase = lambda d: pl.multiple_of(mod(y + d, 4) * 96, 96)
    qbase = lambda v, core, d: 41 * core + ND[v] + NQ[v] * mod(x + d, 4)

    def base(v, g, core, d=0):
        return qbase(v, core, d) if g == "q" else 41 * core + chunks[v][g][0]

    def assemble(v, g):
        lo, count = chunks[v][g]
        blocks = [zbs[v][:, lo + n].reshape(128, 128) for n in range(count)]
        rows = jnp.dot(
            squeeze, jnp.concatenate(blocks, axis=1), preferred_element_type=F32
        ).astype(BF)
        first = base(v, g, c)
        for n in range(count):
            ws[v][first + n, pl.ds(ybase(0), 96), :] = rows[:, 128 * n : 128 * n + 128]

    def yview(v, g, d, part, core=None):
        lo, n = split(v, g, part)
        lo = lo - chunks[v][g][0]
        first = base(v, g, c if core is None else core) + lo
        return ws[v].at[pl.ds(first, n), pl.ds(ybase(d), 96), :]

    def ystart(v, g):
        send(("yf1", v, g), yview(v, g, 0, 0), ydev(1))
        send(("yb1", v, g), yview(v, g, 0, 0), ydev(-1))
        yhand(v, g, 0)

    def ypass(v, g):
        recv(("yf1", v, g), yview(v, g, -1, 0))
        send(("yf2", v, g), yview(v, g, -1, 1), ydev(1), when=z != 0)
        recv(("yb1", v, g), yview(v, g, 1, 0))
        send(("yb2", v, g), yview(v, g, 1, 2), ydev(-1), when=z != 7)
        yhand(v, g, -1)
        yhand(v, g, 1)

    def ywait(v, g):
        recv(("yf2", v, g), yview(v, g, -2, 1), z != 0)
        send(("ye1", v, g), yview(v, g, -2, 1), zdev(-1), when=z == 1)
        recv(("yb2", v, g), yview(v, g, 2, 2), z != 7)
        send(("ye2", v, g), yview(v, g, 2, 2), zdev(1), when=z == 6)
        recv(("ye1", v, g), yview(v, g, -2, 1), z == 0)
        recv(("ye2", v, g), yview(v, g, 2, 2), z == 7)
        yhand(v, g, 2)

    def yhand(v, g, d):
        if g != "q":
            send(("h", v, g, d), yview(v, g, d, 0), pair)

    def xview(v, d, part):
        lo, n = ((0, 1), (1, NQ[v] - 1))[part - 1]
        return ws[v].at[pl.ds(qbase(v, c, d) + lo, n)]

    def xstart(v):
        for first in (1, 2):
            send(("xf", v, first), xview(v, 0, first), xdev(1))
            send(("xb", v, 3 - first), xview(v, 0, 3 - first), xdev(-1))

    def xpass(v, d):
        key, part = ("xf", 1) if d > 0 else ("xb", 2)
        recv((key, v, part), xview(v, -d, part))
        send((key, v, 3), xview(v, -d, part), xdev(d))

    def xsides(v):
        recv(("xf", v, 2), xview(v, -1, 2))
        recv(("xb", v, 1), xview(v, 1, 1))

    def xwait(v):
        recv(("xf", v, 3), xview(v, -2, 1))
        recv(("xb", v, 3), xview(v, 2, 2))

    def cview(v, core, d):
        return ws[v].at[pl.ds(qbase(v, core, d), NQ[v])]

    def hand(v, g, d):
        send(("c", v, g, d), cview(v, c, d), pair)

    def taken(v, g):
        for d in (0, -1, 1, 2):
            recv(("h", v, g, d), yview(v, g, d, 0, 1 - c))

    def alltaken(v):
        for d in (0, 1, -1, 2):
            recv(("c", v, "q", d), cview(v, 1 - c, d))

    def normed(v, values):
        scale = lax.rsqrt(jnp.mean(values * values, axis=-1, keepdims=True) + 1e-06)
        return jax.nn.silu(values * scale * gains[v][...].reshape(1, C)).astype(BF)

    inner_lo, inner_hi, later, first = r > 0, r < 31, tm < 7, tm == 0

    def halo_row(v):
        xs = xss[v]
        own = xs.at[1, 1, pl.ds(2, 2)]
        send(("t1", v), own, tdev(1), xs.at[1, 1, pl.ds(0, 2)], later)

    def halo_start(v):
        xs = xss[v]
        own = xs.at[1, 1, pl.ds(2, 2)]
        send(("up", v), own, rdev(1), xs.at[1, 0, pl.ds(2, 2)], inner_hi)
        send(("dn", v), own, rdev(-1), xs.at[1, 2, pl.ds(2, 2)], inner_lo)
        away = later & (c == 1)
        below, above = (mod(tm + 1, 8), mod(r + 1, 32)), (mod(tm + 1, 8), mod(r - 1, 32))
        send(("t0", v), own, below, xs.at[1, 0, pl.ds(0, 2)], away & inner_hi)
        send(("t2", v), own, above, xs.at[1, 2, pl.ds(0, 2)], away & inner_lo)

    def cache_start(v):
        xs = xss[v]

        @pl.when(first)
        def _():
            xs[1, 1, 0:2] = caches[v][...]

        old = xs.at[1, 1, pl.ds(0, 2)]
        send(("cu", v), old, rdev(1), xs.at[1, 0, pl.ds(0, 2)], first & inner_hi)
        send(("cn", v), old, rdev(-1), xs.at[1, 2, pl.ds(0, 2)], first & inner_lo)

        @pl.when(r == 0)
        def _():
            xs[1, 0] = jnp.zeros((4, W, C), BF)

        @pl.when(r == 31)
        def _():
            xs[1, 2] = jnp.zeros((4, W, C), BF)

    def halo_pass(v):
        xs = xss[v]
        low, high = xs.at[1, 0, pl.ds(2, 2)], xs.at[1, 2, pl.ds(2, 2)]
        recv(("up", v), low, inner_lo)
        send(("t0", v), low, tdev(1), xs.at[1, 0, pl.ds(0, 2)], (c == 0) & inner_lo)
        recv(("dn", v), high, inner_hi)
        send(("t2", v), high, tdev(1), xs.at[1, 2, pl.ds(0, 2)], (c == 0) & inner_hi)

    def halo_wait(v):
        xs = xss[v]
        old = [xs.at[1, j, pl.ds(0, 2)] for j in range(3)]
        recv(("t1", v), old[1], tm > 0)
        recv(("t0", v), old[0], (tm > 0) & inner_lo)
        recv(("t2", v), old[2], (tm > 0) & inner_hi)
        recv(("cu", v), old[0], first & inner_lo)
        recv(("cn", v), old[2], first & inner_hi)

    def shift(buf, j, f):
        v = buf[1, j, f].astype(F32)
        at = lax.broadcasted_iota(jnp.int32, v.shape, 0)
        buf[0, j, f] = jnp.where(at == 0, 0.0, pltpu.roll(v, 1, 0)).astype(BF)
        buf[2, j, f] = jnp.where(at == W - 1, 0.0, pltpu.roll(v, W - 1, 0)).astype(BF)

    def shifts(buf, js, f0, n):
        for j in js:

            def body(f, _):
                shift(buf, j, f0 + f)
                return 0

            lax.fori_loop(0, n, body, 0)

    def conv(v, *pieces):
        xs, w = xss[v], ws[v]

        def pick(n):
            ij = jnp.int32(pieces[0])
            for m in range(1, len(pieces)):
                ij = jnp.where(n == m, pieces[m], ij)
            return ij

        def add(*several):
            lhs, rhs = [], []
            for ij in several:
                i, j = ij // 3, ij % 3
                low = 9 * ij - jnp.where((ij == 5) | (ij == 6), 4, 0)
                high = low + jnp.where(ij == 4, 18, 0)
                lhs += [xs[k, j, pl.ds(i, 2)].reshape(2 * W, C) for k in range(3)]
                rhs += [w[(low if u < 5 else high) + u] for u in range(9)]
            acc[...] += lax.dot_general(
                jnp.concatenate(lhs, axis=1),
                jnp.concatenate(rhs, axis=1),
                NT,
                preferred_element_type=F32,
            )

        def body(n, _):
            add(pick(2 * n), pick(2 * n + 1))
            return 0

        lax.fori_loop(0, len(pieces) // 2, body, 0)
        if len(pieces) % 2:
            add(jnp.int32(pieces[-1]))

    def combine():
        for a in range(2):
            for p in range(2):
                for b in range(2):
                    for q in range(2):
                        total = sum(
                            up[j, k].astype(F32) for j in TAPS[a][p] for k in TAPS[b][q]
                        )
                        cw[a, p, b, q] = total.astype(BF)

    def phase(a, b, p):
        lhs = jnp.concatenate(
            [bs[b + q, a + p].reshape(2 * W, C) for q in range(2)], axis=1
        )
        rhs = jnp.concatenate([cw[a, p, b, q] for q in range(2)], axis=1)
        return lax.dot_general(lhs, rhs, NT, preferred_element_type=F32)

    barrier = pltpu.get_barrier_semaphore()
    near = [f(d) for f in (zdev, ydev, xdev, tdev, rdev) for d in (1, -1)]
    near += [zdev(2), zdev(-2)]
    near += [(mod(tm + d, 8), mod(r + e, 32)) for d in (1, -1) for e in (1, -1)]
    for dev in near:
        pl.semaphore_signal(barrier, inc=1, device_id=dev, device_id_type=pl.DeviceIdType.MESH)
    prepare(0)
    pl.semaphore_wait(barrier, len(near))

    zstart(0, "q")
    xs0[1, 1, 2:4] = normed(0, frames[...].astype(F32).reshape(2 * W, C)).reshape(2, W, C)
    halo_row(0)
    zpass(0, "q")
    zstart(0, "b")
    zstart(0, "c")
    zwait(0, "q")
    assemble(0, "q")
    ystart(0, "q")
    zpass(0, "b")
    prepare(1)
    zpass(0, "c")
    zwait(0, "b")
    assemble(0, "b")
    ypass(0, "q")
    ystart(0, "b")
    zwait(0, "c")
    assemble(0, "c")
    ystart(0, "c")
    ywait(0, "q")
    xstart(0)
    hand(0, "q", 0)
    zstart(1, "q")
    zstart(1, "b")
    halo_start(0)
    cache_start(0)
    zstart(1, "r")
    ypass(0, "b")
    xpass(0, 1)
    zpass(1, "q")
    zpass(1, "b")
    shifts(xs0, (1,), 2, 2)
    ypass(0, "c")
    zwait(1, "q")
    assemble(1, "q")
    ystart(1, "q")
    xpass(0, -1)
    ywait(0, "b")
    halo_pass(0)
    zwait(1, "b")
    assemble(1, "b")
    ystart(1, "b")
    ywait(0, "c")
    xsides(0)
    hand(0, "q", 1)
    hand(0, "q", -1)
    zpass(1, "r")
    ypass(1, "q")
    acc[...] = jnp.zeros_like(acc)
    halo_wait(0)
    shifts(xs0, (0, 2), 2, 2)
    shifts(xs0, (0, 1, 2), 0, 2)
    taken(0, "b")
    conv(0, 0, 5)
    xwait(0)
    hand(0, "q", 2)
    ywait(1, "q")
    taken(0, "c")
    conv(0, 1, 6)
    zwait(1, "r")
    assemble(1, "c")
    ystart(1, "c")
    assemble(1, "e")
    ystart(1, "e")
    ypass(1, "b")
    alltaken(0)
    conv(0, 2, 3, 4, 7, 8)
    xs1[1, 1, 2:4] = normed(1, acc[...].astype(BF).astype(F32)).reshape(2, W, C)
    halo_row(1)
    halo_start(1)
    cache_start(1)
    xstart(1)
    hand(1, "q", 0)
    ypass(1, "c")
    xpass(1, 1)
    acc[...] = frames[...].astype(F32).reshape(2 * W, C)
    shifts(xs1, (1,), 2, 2)
    xpass(1, -1)
    combine()
    ywait(1, "b")
    xsides(1)
    hand(1, "q", 1)
    hand(1, "q", -1)
    halo_pass(1)
    ypass(1, "e")
    xwait(1)
    hand(1, "q", 2)
    ywait(1, "c")
    halo_wait(1)
    shifts(xs1, (0, 2), 2, 2)
    shifts(xs1, (0, 1, 2), 0, 2)
    taken(1, "b")
    conv(1, 0, 5)
    ywait(1, "e")
    taken(1, "c")
    conv(1, 1, 6)
    alltaken(1)
    conv(1, 3, 8)
    taken(1, "e")
    conv(1, 2, 4, 7)

    bs[1, 1] = acc[...].astype(BF).reshape(2, W, C)
    send("bu", bs.at[1, 1], rdev(1), bs.at[1, 0], inner_hi)
    send("bd", bs.at[1, 1], rdev(-1), bs.at[1, 2], inner_lo)

    @pl.when(r == 0)
    def _():
        bs[1, 0] = jnp.zeros((2, W, C), BF)

    @pl.when(r == 31)
    def _():
        bs[1, 2] = jnp.zeros((2, W, C), BF)

    shifts(bs, (1,), 0, 2)
    for a in range(2):
        for b in range(2):
            ph[a, b] = phase(a, b, 1 - a)
    recv("bu", bs.at[1, 0], inner_lo)
    recv("bd", bs.at[1, 2], inner_hi)
    shifts(bs, (0, 2), 0, 2)
    for a in range(2):
        for b in range(2):
            total = ph[a, b] + phase(a, b, a)
            for f in range(2):
                part = total[f * W : (f + 1) * W]
                il[f, pl.ds(b, W, stride=2), :] = part[:, :128]
                il[2 + f, pl.ds(b, W, stride=2), 0:64] = part[:, 128:]
        for f in range(2):
            out[f, a, :, 0:128] = il[f].astype(BF)
            out[f, a, :, 128:192] = il[2 + f, :, 0:64].astype(BF)

    for key, src, dst, dev, when in sends:
        done = lambda k=key, s=src, d=dst, e=dev: copy(k, s, d, e).wait_send()
        if when is None:
            done()
        else:
            pl.when(when)(done)


def shards(frames, cache0, cache1, gain0, gain1, first, second, upsample):
    vmem = pl.BlockSpec(memory_space=pltpu.VMEM)
    block = lambda v: v.reshape(2, W, C)
    flip = lambda v: jnp.swapaxes(v, 3, 4).reshape(27, 12, C)
    return pl.pallas_call(
        kernel,
        out_shape=jax.ShapeDtypeStruct((2, 2, 2 * W, CO), BF),
        in_specs=[vmem] * 8,
        out_specs=vmem,
        scratch_shapes=[
            pltpu.VMEM((8, ND[0] + NQ[0], 16, 128), BF),
            pltpu.VMEM((8, ND[1] + NQ[1], 16, 128), BF),
            pltpu.VMEM((2 * NC, C, 128), BF),
            pltpu.VMEM((2 * NC, C, 128), BF),
            pltpu.VMEM((3, 3, 4, W, C), BF),
            pltpu.VMEM((3, 3, 4, W, C), BF),
            pltpu.VMEM((3, 3, 2, W, C), BF),
            pltpu.VMEM((2 * W, C), F32),
            pltpu.VMEM((2, 2, 2, 2, CO, C), BF),
            pltpu.VMEM((2, 2, 2 * W, CO), F32),
            pltpu.VMEM((4, 2 * W, 128), F32),
            pltpu.SemaphoreType.DMA((176,)),
            pltpu.SemaphoreType.DMA((176,)),
        ],
        compiler_params=pltpu.CompilerParams(
            collective_id=0, has_side_effects=True, vmem_limit_bytes=60 << 20
        ),
    )(
        block(frames),
        block(cache0),
        block(cache1),
        gain0,
        gain1,
        flip(first),
        flip(second),
        jnp.swapaxes(upsample, 2, 3),
    )


def solution(mesh):
    in_specs = (
        P("tm", "rows", None, None),
        P(None, "rows", None, None),
        P(None, "rows", None, None),
        P(),
        P(),
        P(None, None, None, None, "rows"),
        P(None, None, None, None, "rows"),
        P(),
    )
    out_specs = P("tm", "rows", None, None)
    return jax.shard_map(shards, mesh=mesh, in_specs=in_specs, out_specs=out_specs, check_vma=False)
```

```python
import jax
import jax.numpy as jnp
from jax import lax
from jax.experimental import pallas as pl
from jax.experimental.pallas import tpu as pltpu
from jax.sharding import PartitionSpec as P

BF = jnp.bfloat16
F32 = jnp.float32
NT = (((1,), (1,)), ((), ()))
W = 160
C = 384
CO = 192
ND = (25, 29)
NQ = (4, 3)
NC = 41
NB = 9
CUTS = ((16, 0), (9, 11))
TAPS = (((0,), (1, 2)), ((0, 1), (2,)))


def mod(a, n):
    return lax.rem(a + n, n)


def kernel(
    frames,
    cache0,
    cache1,
    gain0,
    gain1,
    win0,
    win1,
    up,
    out,
    zb0,
    zb1,
    w0,
    w1,
    xs0,
    xs1,
    bs,
    acc,
    cw,
    ph,
    il,
    ssem,
    rsem,
):
    tm = lax.axis_index("tm")
    r = lax.axis_index("rows")
    x, c = tm // 2, tm % 2
    y, z = r // 8, r % 8
    zdev = lambda d: (tm, y * 8 + mod(z + d, 8))
    ydev = lambda d: (tm, mod(y + d, 4) * 8 + z)
    xdev = lambda d: (mod(x + d, 4) * 2 + c, r)
    tdev = lambda d: (mod(tm + d, 8), r)
    rdev = lambda d: (tm, mod(r + d, 32))
    pair = (x * 2 + 1 - c, r)

    index = {}
    sends = []

    def copy(key, src, dst, dev):
        n = index.setdefault(key, len(index))
        return pltpu.make_async_remote_copy(
            src_ref=src,
            dst_ref=dst,
            send_sem=ssem.at[n],
            recv_sem=rsem.at[n],
            device_id=dev,
            device_id_type=pl.DeviceIdType.MESH,
        )

    def send(key, src, dev, dst=None, when=None):
        dst = src if dst is None else dst

        def go():
            copy(key, src, dst, dev).start()

        if when is None:
            go()
        else:
            pl.when(when)(go)
        sends.append((key, src, dst, dev, when))

    def recv(key, dst, when=None):
        def go():
            copy(key, dst, dst, pair).wait_recv()

        if when is None:
            go()
        else:
            pl.when(when)(go)

    zbs, ws, wins, xss = (zb0, zb1), (w0, w1), (win0, win1), (xs0, xs1)
    caches, gains = (cache0, cache1), (gain0, gain1)

    chunks = []
    for d, q, (nc, ne) in zip(ND, NQ, CUTS):
        chunks.append(
            {
                "b": (0, NB),
                "c": (NB, nc),
                "e": (NB + nc, ne),
                "r": (NB, nc + ne),
                "q": (d, q),
            }
        )

    def unit(v, n):
        local = jnp.where(n < ND[v], n, n + NQ[v] * x)
        second = jnp.where(
            local < 18,
            45 + local,
            jnp.where(
                local < 21,
                23 + local,
                jnp.where(local == 21, 44, jnp.where(local == 40, 40, 41 + local)),
            ),
        )
        return jnp.where(c == 0, local, second)

    def prepare(v):
        zb, win = zbs[v], wins[v]
        zb[z] = jnp.zeros((ND[v] + NQ[v], 16, 128), BF)

        def body(n, _):
            u = unit(v, n)
            lane = pl.multiple_of((u % 3) * 128, 128)
            zb[z, n, 0:12, :] = win[u // 3, :, pl.ds(lane, 128)]
            return 0

        lax.fori_loop(0, ND[v] + NQ[v], body, 0)

    def split(v, g, part):
        lo, n = chunks[v][g]
        cut = (n + 1) // 2
        return ((lo, n), (lo, cut), (lo + cut, n - cut))[part]

    def zview(v, g, d, part=0):
        return zbs[v].at[mod(z + d, 8), pl.ds(*split(v, g, part))]

    def zstart(v, g):
        for d in (2, -2, 1, -1):
            send(("z", v, g, d), zview(v, g, 0), zdev(d))

    def zpass(v, g):
        for d in (2, -2):
            part = 1 if d > 0 else 2
            recv(("z", v, g, d), zview(v, g, -d))
            send(("z", v, g, 2 * d), zview(v, g, -d, part), zdev(d))
            send(("z", v, g, 3 * d // 2), zview(v, g, -d), zdev(d // 2))

    def zwait(v, g):
        for d in (1, -1, 3, -3):
            recv(("z", v, g, d), zview(v, g, -d))
        for d in (4, -4):
            recv(("z", v, g, d), zview(v, g, -d, 1 if d > 0 else 2))

    row = lax.broadcasted_iota(jnp.int32, (96, 128), 0)
    col = lax.broadcasted_iota(jnp.int32, (96, 128), 1)
    squeeze = jnp.where(row + 4 * (row // 12) == col, 1.0, 0.0).astype(BF)
    ybase = lambda d: pl.multiple_of(mod(y + d, 4) * 96, 96)
    qbase = lambda v, core, d: 41 * core + ND[v] + NQ[v] * mod(x + d, 4)

    def base(v, g, core, d=0):
        return qbase(v, core, d) if g == "q" else 41 * core + chunks[v][g][0]

    def assemble(v, g):
        lo, count = chunks[v][g]
        blocks = [zbs[v][:, lo + n].reshape(128, 128) for n in range(count)]
        rows = jnp.dot(
            squeeze, jnp.concatenate(blocks, axis=1), preferred_element_type=F32
        ).astype(BF)
        first = base(v, g, c)
        for n in range(count):
            ws[v][first + n, pl.ds(ybase(0), 96), :] = rows[:, 128 * n : 128 * n + 128]

    def yview(v, g, d, part, core=None):
        lo, n = split(v, g, part)
        lo = lo - chunks[v][g][0]
        first = base(v, g, c if core is None else core) + lo
        return ws[v].at[pl.ds(first, n), pl.ds(ybase(d), 96), :]

    def ystart(v, g):
        send(("yf1", v, g), yview(v, g, 0, 0), ydev(1))
        send(("yb1", v, g), yview(v, g, 0, 0), ydev(-1))
        yhand(v, g, 0)

    def ypass(v, g):
        recv(("yf1", v, g), yview(v, g, -1, 0))
        send(("yf2", v, g), yview(v, g, -1, 1), ydev(1), when=z != 0)
        recv(("yb1", v, g), yview(v, g, 1, 0))
        send(("yb2", v, g), yview(v, g, 1, 2), ydev(-1), when=z != 7)
        yhand(v, g, -1)
        yhand(v, g, 1)

    def ywait(v, g):
        recv(("yf2", v, g), yview(v, g, -2, 1), z != 0)
        send(("ye1", v, g), yview(v, g, -2, 1), zdev(-1), when=z == 1)
        recv(("yb2", v, g), yview(v, g, 2, 2), z != 7)
        send(("ye2", v, g), yview(v, g, 2, 2), zdev(1), when=z == 6)
        recv(("ye1", v, g), yview(v, g, -2, 1), z == 0)
        recv(("ye2", v, g), yview(v, g, 2, 2), z == 7)
        yhand(v, g, 2)

    def yhand(v, g, d):
        if g != "q":
            send(("h", v, g, d), yview(v, g, d, 0), pair)

    def xview(v, d, part):
        lo, n = ((0, 1), (1, NQ[v] - 1))[part - 1]
        return ws[v].at[pl.ds(qbase(v, c, d) + lo, n)]

    def xstart(v):
        for first in (1, 2):
            send(("xf", v, first), xview(v, 0, first), xdev(1))
            send(("xb", v, 3 - first), xview(v, 0, 3 - first), xdev(-1))

    def xpass(v, d):
        key, part = ("xf", 1) if d > 0 else ("xb", 2)
        recv((key, v, part), xview(v, -d, part))
        send((key, v, 3), xview(v, -d, part), xdev(d))

    def xsides(v):
        recv(("xf", v, 2), xview(v, -1, 2))
        recv(("xb", v, 1), xview(v, 1, 1))

    def xwait(v):
        recv(("xf", v, 3), xview(v, -2, 1))
        recv(("xb", v, 3), xview(v, 2, 2))

    def cview(v, core, d):
        return ws[v].at[pl.ds(qbase(v, core, d), NQ[v])]

    def hand(v, g, d):
        send(("c", v, g, d), cview(v, c, d), pair)

    def taken(v, g):
        for d in (0, -1, 1, 2):
            recv(("h", v, g, d), yview(v, g, d, 0, 1 - c))

    def alltaken(v):
        for d in (0, 1, -1, 2):
            recv(("c", v, "q", d), cview(v, 1 - c, d))

    def normed(v, values):
        scale = lax.rsqrt(jnp.mean(values * values, axis=-1, keepdims=True) + 1e-06)
        return jax.nn.silu(values * scale * gains[v][...].reshape(1, C)).astype(BF)

    inner_lo, inner_hi, later, first = r > 0, r < 31, tm < 7, tm == 0

    def halo_row(v):
        xs = xss[v]
        own = xs.at[1, 1, pl.ds(2, 2)]
        send(("t1", v), own, tdev(1), xs.at[1, 1, pl.ds(0, 2)], later)

    def halo_start(v):
        xs = xss[v]
        own = xs.at[1, 1, pl.ds(2, 2)]
        send(("up", v), own, rdev(1), xs.at[1, 0, pl.ds(2, 2)], inner_hi)
        send(("dn", v), own, rdev(-1), xs.at[1, 2, pl.ds(2, 2)], inner_lo)
        away = later & (c == 1)
        below, above = (mod(tm + 1, 8), mod(r + 1, 32)), (mod(tm + 1, 8), mod(r - 1, 32))
        send(("t0", v), own, below, xs.at[1, 0, pl.ds(0, 2)], away & inner_hi)
        send(("t2", v), own, above, xs.at[1, 2, pl.ds(0, 2)], away & inner_lo)

    def cache_start(v):
        xs = xss[v]

        @pl.when(first)
        def _():
            xs[1, 1, 0:2] = caches[v][...]

        old = xs.at[1, 1, pl.ds(0, 2)]
        send(("cu", v), old, rdev(1), xs.at[1, 0, pl.ds(0, 2)], first & inner_hi)
        send(("cn", v), old, rdev(-1), xs.at[1, 2, pl.ds(0, 2)], first & inner_lo)

        @pl.when(r == 0)
        def _():
            xs[1, 0] = jnp.zeros((4, W, C), BF)

        @pl.when(r == 31)
        def _():
            xs[1, 2] = jnp.zeros((4, W, C), BF)

    def halo_pass(v):
        xs = xss[v]
        low, high = xs.at[1, 0, pl.ds(2, 2)], xs.at[1, 2, pl.ds(2, 2)]
        recv(("up", v), low, inner_lo)
        send(("t0", v), low, tdev(1), xs.at[1, 0, pl.ds(0, 2)], (c == 0) & inner_lo)
        recv(("dn", v), high, inner_hi)
        send(("t2", v), high, tdev(1), xs.at[1, 2, pl.ds(0, 2)], (c == 0) & inner_hi)

    def halo_wait(v):
        xs = xss[v]
        old = [xs.at[1, j, pl.ds(0, 2)] for j in range(3)]
        recv(("t1", v), old[1], tm > 0)
        recv(("t0", v), old[0], (tm > 0) & inner_lo)
        recv(("t2", v), old[2], (tm > 0) & inner_hi)
        recv(("cu", v), old[0], first & inner_lo)
        recv(("cn", v), old[2], first & inner_hi)

    def shift(buf, j, f):
        v = buf[1, j, f].astype(F32)
        at = lax.broadcasted_iota(jnp.int32, v.shape, 0)
        buf[0, j, f] = jnp.where(at == 0, 0.0, pltpu.roll(v, 1, 0)).astype(BF)
        buf[2, j, f] = jnp.where(at == W - 1, 0.0, pltpu.roll(v, W - 1, 0)).astype(BF)

    def shifts(buf, js, f0, n):
        for j in js:

            def body(f, _):
                shift(buf, j, f0 + f)
                return 0

            lax.fori_loop(0, n, body, 0)

    def conv(v, *pieces):
        xs, w = xss[v], ws[v]

        def body(n, _):
            ij = jnp.int32(pieces[0])
            for m in range(1, len(pieces)):
                ij = jnp.where(n == m, pieces[m], ij)
            i, j = ij // 3, ij % 3
            low = 9 * ij - jnp.where((ij == 5) | (ij == 6), 4, 0)
            high = low + jnp.where(ij == 4, 18, 0)
            lhs = jnp.concatenate(
                [xs[k, j, pl.ds(i, 2)].reshape(2 * W, C) for k in range(3)], axis=1
            )
            rhs = jnp.concatenate([w[(low if u < 5 else high) + u] for u in range(9)], axis=1)
            acc[...] += lax.dot_general(lhs, rhs, NT, preferred_element_type=F32)
            return 0

        lax.fori_loop(0, len(pieces), body, 0)

    def combine():
        for a in range(2):
            for p in range(2):
                for b in range(2):
                    for q in range(2):
                        total = sum(
                            up[j, k].astype(F32) for j in TAPS[a][p] for k in TAPS[b][q]
                        )
                        cw[a, p, b, q] = total.astype(BF)

    def phase(a, b, p):
        lhs = jnp.concatenate(
            [bs[b + q, a + p].reshape(2 * W, C) for q in range(2)], axis=1
        )
        rhs = jnp.concatenate([cw[a, p, b, q] for q in range(2)], axis=1)
        return lax.dot_general(lhs, rhs, NT, preferred_element_type=F32)

    barrier = pltpu.get_barrier_semaphore()
    near = [f(d) for f in (zdev, ydev, xdev, tdev, rdev) for d in (1, -1)]
    near += [zdev(2), zdev(-2)]
    near += [(mod(tm + d, 8), mod(r + e, 32)) for d in (1, -1) for e in (1, -1)]
    for dev in near:
        pl.semaphore_signal(barrier, inc=1, device_id=dev, device_id_type=pl.DeviceIdType.MESH)
    prepare(0)
    pl.semaphore_wait(barrier, len(near))

    zstart(0, "q")
    xs0[1, 1, 2:4] = normed(0, frames[...].astype(F32).reshape(2 * W, C)).reshape(2, W, C)
    halo_row(0)
    zpass(0, "q")
    zstart(0, "b")
    zstart(0, "c")
    zwait(0, "q")
    assemble(0, "q")
    ystart(0, "q")
    zpass(0, "b")
    prepare(1)
    zpass(0, "c")
    zwait(0, "b")
    assemble(0, "b")
    ypass(0, "q")
    ystart(0, "b")
    zwait(0, "c")
    assemble(0, "c")
    ystart(0, "c")
    ywait(0, "q")
    xstart(0)
    hand(0, "q", 0)
    zstart(1, "q")
    zstart(1, "b")
    halo_start(0)
    cache_start(0)
    zstart(1, "r")
    ypass(0, "b")
    xpass(0, 1)
    zpass(1, "q")
    zpass(1, "b")
    shifts(xs0, (1,), 2, 2)
    ypass(0, "c")
    zwait(1, "q")
    assemble(1, "q")
    ystart(1, "q")
    xpass(0, -1)
    ywait(0, "b")
    halo_pass(0)
    zwait(1, "b")
    assemble(1, "b")
    ystart(1, "b")
    ywait(0, "c")
    xsides(0)
    hand(0, "q", 1)
    hand(0, "q", -1)
    zpass(1, "r")
    ypass(1, "q")
    acc[...] = jnp.zeros_like(acc)
    halo_wait(0)
    shifts(xs0, (0, 2), 2, 2)
    shifts(xs0, (0, 1, 2), 0, 2)
    taken(0, "b")
    conv(0, 0, 5)
    xwait(0)
    hand(0, "q", 2)
    ywait(1, "q")
    xstart(1)
    hand(1, "q", 0)
    taken(0, "c")
    conv(0, 1, 6)
    zwait(1, "r")
    assemble(1, "c")
    ystart(1, "c")
    assemble(1, "e")
    ystart(1, "e")
    ypass(1, "b")
    alltaken(0)
    conv(0, 2, 3, 4, 7, 8)
    xs1[1, 1, 2:4] = normed(1, acc[...].astype(BF).astype(F32)).reshape(2, W, C)
    halo_row(1)
    halo_start(1)
    cache_start(1)
    xpass(1, 1)
    acc[...] = frames[...].astype(F32).reshape(2 * W, C)
    shifts(xs1, (1,), 2, 2)
    xpass(1, -1)
    ypass(1, "c")
    combine()
    ywait(1, "b")
    xsides(1)
    hand(1, "q", 1)
    hand(1, "q", -1)
    halo_pass(1)
    ypass(1, "e")
    xwait(1)
    hand(1, "q", 2)
    ywait(1, "c")
    halo_wait(1)
    shifts(xs1, (0, 2), 2, 2)
    shifts(xs1, (0, 1, 2), 0, 2)
    taken(1, "b")
    conv(1, 0, 5)
    ywait(1, "e")
    taken(1, "c")
    conv(1, 1, 6)
    alltaken(1)
    conv(1, 8)
    taken(1, "e")
    conv(1, 2, 3, 4, 7)

    bs[1, 1] = acc[...].astype(BF).reshape(2, W, C)
    send("bu", bs.at[1, 1], rdev(1), bs.at[1, 0], inner_hi)
    send("bd", bs.at[1, 1], rdev(-1), bs.at[1, 2], inner_lo)

    @pl.when(r == 0)
    def _():
        bs[1, 0] = jnp.zeros((2, W, C), BF)

    @pl.when(r == 31)
    def _():
        bs[1, 2] = jnp.zeros((2, W, C), BF)

    shifts(bs, (1,), 0, 2)
    for a in range(2):
        for b in range(2):
            ph[a, b] = phase(a, b, 1 - a)
    recv("bu", bs.at[1, 0], inner_lo)
    recv("bd", bs.at[1, 2], inner_hi)
    shifts(bs, (0, 2), 0, 2)
    for a in range(2):
        for b in range(2):
            total = ph[a, b] + phase(a, b, a)
            for f in range(2):
                part = total[f * W : (f + 1) * W]
                il[f, pl.ds(b, W, stride=2), :] = part[:, :128]
                il[2 + f, pl.ds(b, W, stride=2), 0:64] = part[:, 128:]
        for f in range(2):
            out[f, a, :, 0:128] = il[f].astype(BF)
            out[f, a, :, 128:192] = il[2 + f, :, 0:64].astype(BF)

    for key, src, dst, dev, when in sends:
        done = lambda k=key, s=src, d=dst, e=dev: copy(k, s, d, e).wait_send()
        if when is None:
            done()
        else:
            pl.when(when)(done)


def shards(frames, cache0, cache1, gain0, gain1, first, second, upsample):
    vmem = pl.BlockSpec(memory_space=pltpu.VMEM)
    block = lambda v: v.reshape(2, W, C)
    flip = lambda v: jnp.swapaxes(v, 3, 4).reshape(27, 12, C)
    return pl.pallas_call(
        kernel,
        out_shape=jax.ShapeDtypeStruct((2, 2, 2 * W, CO), BF),
        in_specs=[vmem] * 8,
        out_specs=vmem,
        scratch_shapes=[
            pltpu.VMEM((8, ND[0] + NQ[0], 16, 128), BF),
            pltpu.VMEM((8, ND[1] + NQ[1], 16, 128), BF),
            pltpu.VMEM((2 * NC, C, 128), BF),
            pltpu.VMEM((2 * NC, C, 128), BF),
            pltpu.VMEM((3, 3, 4, W, C), BF),
            pltpu.VMEM((3, 3, 4, W, C), BF),
            pltpu.VMEM((3, 3, 2, W, C), BF),
            pltpu.VMEM((2 * W, C), F32),
            pltpu.VMEM((2, 2, 2, 2, CO, C), BF),
            pltpu.VMEM((2, 2, 2 * W, CO), F32),
            pltpu.VMEM((4, 2 * W, 128), F32),
            pltpu.SemaphoreType.DMA((176,)),
            pltpu.SemaphoreType.DMA((176,)),
        ],
        compiler_params=pltpu.CompilerParams(
            collective_id=0, has_side_effects=True, vmem_limit_bytes=60 << 20
        ),
    )(
        block(frames),
        block(cache0),
        block(cache1),
        gain0,
        gain1,
        flip(first),
        flip(second),
        jnp.swapaxes(upsample, 2, 3),
    )


def solution(mesh):
    in_specs = (
        P("tm", "rows", None, None),
        P(None, "rows", None, None),
        P(None, "rows", None, None),
        P(),
        P(),
        P(None, None, None, None, "rows"),
        P(None, None, None, None, "rows"),
        P(),
    )
    out_specs = P("tm", "rows", None, None)
    return jax.shard_map(shards, mesh=mesh, in_specs=in_specs, out_specs=out_specs, check_vma=False)
```
